512 devices in a mesh: expert: 128 (over z, x, core), rep: 4 (over y).
Axes of the slice: x: 4, y: 4, z: 16, core: 2. Of those that a mesh axis runs over, the one named last changes fastest.
Arguments:
- tokens: bfloat16 [512, 256, 1280], P(('rep', 'expert')), parts along dimension 0, may hold values from -48 to 48, as said below
- slot_weight: bfloat16 [5120, 16], P('rep'), parts along dimension 0, may hold values from -1 to 1, as said below
- w_in: bfloat16 [1280, 81920], P(None, 'expert'), may hold values from -0.15625 to 0.15625
- w_out: bfloat16 [81920, 1280], P('expert'), may hold values from -0.078125 to 0.078125
Outputs:
- mixed: bfloat16 [512, 256, 1280], P(('rep', 'expert')), parts along dimension 0
The draws below stay inside these ranges and needn't reach their ends.
There are 4 independent parts, one for each index of `rep`. The reference program is written for one: setup_inputs(seed, part) draws one part's arguments, and reference() takes and returns one part's arrays. A program takes and returns all parts, laid end to end along the dimension named above; an argument that names none is the same for every part. Nothing has to cross between parts.
Inputs may be any that keep to these rules, and one draw needn't show every extreme that they name: `tokens`: activations mostly of order one. `slot_weight`: entries of deviation 1280 ** -0.5.
All inputs are finite; a program needn't handle non-finite values.
Results may differ from the reference program's by a relative error of at most 0.015.
Values may be sent and summed in bfloat16 or wider, within the bound.
A program may use at most 64 MiB of HBM per device.

```python
import jax
import jax.numpy as jnp
from jax import lax

D = 1280
FF = 5120
PATCHES = 256
HID_DEV = 640
SPLIT = 8
EXPERTS = 16
IMAGES = 128


def router_matrix(key):
    return jnp.clip(jax.random.normal(jax.random.fold_in(key, 7), (D, EXPERTS), jnp.float32), -5.0, 5.0) * D ** (-0.5)


def draw_slot_weight(key, part):
    return router_matrix(key).astype(jnp.bfloat16)


def draw_tokens(key, part):
    key = jax.random.fold_in(key, 3)
    base = jnp.clip(jax.random.normal(jax.random.fold_in(key, 1), (IMAGES, PATCHES, D), jnp.float32), -6.0, 6.0)
    return base.astype(jnp.bfloat16)


def shard_levels(rng, shape, shards, low, largest):
    loudness, own = 1.0, jax.random.fold_in(rng, 6)
    for position, blocks in shards:
        steps = jnp.exp(jax.random.uniform(jax.random.fold_in(own, position), (blocks,), jnp.float32, low / len(shards), largest / len(shards)))
        loudness = loudness * jnp.repeat(steps, shape[position] // blocks).reshape([-1 if axis == position else 1 for axis in range(len(shape))])
    return loudness


def noise(key, dims, width, most, cuts=(), kind=jnp.bfloat16):
    entries = width * jax.random.normal(key, dims, jnp.float32)
    if cuts:
        entries = entries * shard_levels(key, dims, cuts, -0.22, 0.18)
    return jnp.clip(entries, -most, most).astype(kind)


def setup_inputs(seed: int = 0, part: int = 0) -> dict:
    seeds = jax.random.split(jax.random.key(seed), 5)
    own_keys = jax.random.split(jax.random.fold_in(seeds[4], part), 5)
    tokens = draw_tokens(jax.random.fold_in(jax.random.fold_in(seeds[4], part), 71), part)
    slot_weight = draw_slot_weight(jax.random.fold_in(jax.random.fold_in(seeds[4], part), 71), part)
    w_in = noise(seeds[2], (D, EXPERTS * FF), D ** -0.5, 0.15625, ((1, 128),))
    w_out = noise(seeds[3], (EXPERTS * FF, D), FF ** -0.5, 0.078125, ((0, 128),))
    return {"tokens": tokens, "slot_weight": slot_weight, "w_in": w_in, "w_out": w_out}


def reference(tokens, slot_weight, w_in, w_out):
    logits = jnp.einsum("btd,de->bte", tokens.astype(jnp.float32), slot_weight.astype(jnp.float32))
    dispatch = jax.nn.softmax(logits, axis=1).astype(jnp.bfloat16)
    slots = jnp.einsum("bte,btd->bed", dispatch.astype(jnp.float32), tokens.astype(jnp.float32)).astype(jnp.bfloat16)

    def one_expert(index):
        mine = lax.dynamic_index_in_dim(slots, index, 1, keepdims=False)
        first = lax.dynamic_slice_in_dim(w_in, index * FF, FF, 1)
        hidden = jax.nn.gelu(jnp.dot(mine, first, preferred_element_type=jnp.float32)).astype(jnp.bfloat16)
        second = lax.dynamic_slice_in_dim(w_out, index * FF, FF, 0)
        blocks = jnp.einsum("bsh,shd->bsd", hidden.reshape(IMAGES, SPLIT, HID_DEV).astype(jnp.float32),
                            second.reshape(SPLIT, HID_DEV, D).astype(jnp.float32)).astype(jnp.bfloat16)
        return jnp.sum(blocks.astype(jnp.float32), axis=1).astype(jnp.bfloat16)

    expert_out = lax.map(one_expert, jnp.arange(EXPERTS, dtype=jnp.int32))
    combine = jax.nn.softmax(logits, axis=2).astype(jnp.bfloat16)
    mixed = jnp.einsum("bte,ebd->btd", combine.astype(jnp.float32), expert_out.astype(jnp.float32))
    return mixed.astype(jnp.bfloat16)
```

```python
import functools

import jax
import jax.numpy as jnp
from jax import lax
from jax.experimental import pallas as pl
from jax.experimental.pallas import tpu as pltpu
from jax.sharding import PartitionSpec as P

BF16 = jnp.bfloat16
F32 = jnp.float32
CORES = 2


def remote(src, dst, send_sem, recv_sem, target):
    return pltpu.make_async_remote_copy(
        src_ref=src,
        dst_ref=dst,
        send_sem=send_sem,
        recv_sem=recv_sem,
        device_id={"expert": target},
        device_id_type=pl.DeviceIdType.MESH,
    )


def kernel(
    planes,
    columns,
    tokens_hbm,
    slot_ref,
    w_in_hbm,
    w_out_hbm,
    out_ref,
    tokens,
    w_in,
    w_out,
    slot_out,
    slot_in,
    gathered,
    to_core,
    from_core,
    to_column,
    from_column,
    expert_out,
    expert_in,
    load_sem,
    z_send,
    z_recv,
    x_send,
    x_recv,
    c_send,
    c_recv,
):
    side = columns * CORES
    half = columns * planes
    me = lax.axis_index("expert")
    core = lax.rem(me, CORES)
    column = lax.rem(lax.div(me, CORES), columns)
    plane = lax.div(me, side)
    mate = me + 1 - 2 * core

    def in_plane(step):
        return lax.rem(plane + step, planes)

    def at_plane(other):
        return me + (other - plane) * side

    def in_column(step):
        return lax.rem(column + step, columns)

    def at_column(other):
        return me + (other - column) * CORES

    load_tokens = pltpu.make_async_copy(tokens_hbm, tokens, load_sem.at[0])
    load_in = pltpu.make_async_copy(w_in_hbm, w_in, load_sem.at[1])
    load_out = pltpu.make_async_copy(w_out_hbm, w_out, load_sem.at[2])
    load_tokens.start()
    load_in.start()
    load_out.start()
    barrier = pltpu.get_barrier_semaphore()
    peers = [at_plane(in_plane(k)) for k in range(1, planes)]
    peers += [at_column(in_column(k)) for k in range(1, columns)]
    peers += [mate]
    for peer in peers:
        pl.semaphore_signal(
            barrier, inc=1, device_id={"expert": peer}, device_id_type=pl.DeviceIdType.MESH
        )

    load_tokens.wait()
    logits = lax.dot_general(
        slot_ref[...], tokens[0], (((1,), (1,)), ((), ())), preferred_element_type=F32
    )
    top = jnp.max(logits, axis=1, keepdims=True)
    weight = jnp.exp(logits - top)
    dispatch = (weight / jnp.sum(weight, axis=1, keepdims=True)).astype(BF16)
    slots = jnp.dot(dispatch, tokens[0], preferred_element_type=F32)
    slot_out[...] = slots.reshape(slot_out.shape).astype(BF16)

    pl.semaphore_wait(barrier, len(peers))
    order = sorted(range(1, planes), key=lambda k: -min(k, planes - k))
    for k in order:
        to = in_plane(k)
        remote(slot_out.at[to], slot_in.at[plane], z_send.at[0], z_recv.at[0], at_plane(to)).start()
    slot_in[plane] = slot_out[plane]
    top = jnp.max(logits, axis=0, keepdims=True)
    weight = jnp.exp(logits - top)
    combine = (weight / jnp.sum(weight, axis=0, keepdims=True)).astype(BF16)
    arrived = slot_in.at[pl.ds(0, planes - 1)]
    pltpu.make_async_copy(arrived, arrived, z_recv.at[0]).wait()

    def block(c, x):
        return pl.ds(pl.multiple_of((c * columns + x) * planes, planes), planes)

    mine = block(core, column)
    gathered[mine, :] = slot_in[...].reshape(planes, -1)
    first = [
        remote(gathered.at[mine], gathered.at[mine], x_send.at[k], x_recv.at[k], at_column(in_column(k)))
        for k in range(1, columns)
    ]
    for copy in first:
        copy.start()
    relays = [remote(gathered.at[mine], gathered.at[mine], c_send.at[0], c_recv.at[0], mate)]
    relays[0].start()
    for k in range(1, columns):
        came = block(core, in_column(columns - k))
        here = gathered.at[came]
        pltpu.make_async_copy(here, here, x_recv.at[k]).wait()
        relays.append(remote(here, here, c_send.at[k], c_recv.at[k], mate))
        relays[-1].start()
    for relay in relays:
        relay.wait_recv()

    load_in.wait()
    hidden = jnp.dot(gathered[...], w_in[...], preferred_element_type=F32)
    hidden = jax.nn.gelu(hidden).astype(BF16)
    load_out.wait()
    partial_out = jnp.dot(hidden, w_out[...], preferred_element_type=F32)
    is_zero = core == 0
    upper, lower = partial_out[:half], partial_out[half:]
    to_core[...] = jnp.where(is_zero, lower, upper).astype(BF16)
    swap = remote(to_core, from_core, c_send.at[columns], c_recv.at[columns], mate)
    swap.start()
    kept = jnp.where(is_zero, upper, lower)
    swap.wait_recv()
    both = kept + from_core[...].astype(F32)
    to_column[...] = both.reshape(columns, planes, -1).astype(BF16)
    second = []
    for k in range(1, columns):
        to = in_column(k)
        second.append(
            remote(to_column.at[to], from_column.at[k], x_send.at[columns + k], x_recv.at[columns + k], at_column(to))
        )
        second[-1].start()
    total = to_column[column].astype(F32)
    for k in range(1, columns):
        second[k - 1].wait_recv()
        total = total + from_column[k].astype(F32)

    expert_out[...] = total.reshape(expert_out.shape).astype(BF16)
    for k in order:
        to = in_plane(k)
        remote(expert_out.at[to], expert_in.at[plane], z_send.at[1], z_recv.at[1], at_plane(to)).start()
    expert_in[plane] = expert_out[plane]
    arrived = expert_in.at[pl.ds(0, planes - 1)]
    pltpu.make_async_copy(arrived, arrived, z_recv.at[1]).wait()
    mixed = lax.dot_general(
        combine,
        expert_in[...].reshape(planes, -1),
        (((0,), (0,)), ((), ())),
        preferred_element_type=F32,
    )
    out_ref[0] = mixed.astype(BF16)

    for buffer, number in ((slot_out, 0), (expert_out, 1)):
        left = buffer.at[pl.ds(0, planes - 1)]
        pltpu.make_async_copy(left, left, z_send.at[number]).wait()
    for copy in first + relays + [swap] + second:
        copy.wait_send()


def on_device(tokens, slot_weight, w_in, w_out, *, devices, cores_per_chip):
    images, patches, width = tokens.shape
    experts = slot_weight.shape[1]
    units = w_in.shape[1]
    planes = experts
    columns = devices // planes // cores_per_chip
    half = columns * planes
    dma = pltpu.SemaphoreType.DMA
    return pl.pallas_call(
        functools.partial(kernel, planes, columns),
        out_shape=jax.ShapeDtypeStruct(tokens.shape, BF16),
        in_specs=[
            pl.BlockSpec(memory_space=pltpu.HBM),
            pl.BlockSpec(memory_space=pltpu.VMEM),
            pl.BlockSpec(memory_space=pltpu.HBM),
            pl.BlockSpec(memory_space=pltpu.HBM),
        ],
        out_specs=pl.BlockSpec(memory_space=pltpu.VMEM),
        scratch_shapes=[
            pltpu.VMEM(tokens.shape, BF16),
            pltpu.VMEM((width, units), BF16),
            pltpu.VMEM((units, width), BF16),
            pltpu.VMEM((planes, 2, width // 2), BF16),
            pltpu.VMEM((planes, 2, width // 2), BF16),
            pltpu.VMEM((2 * half, width), BF16),
            pltpu.VMEM((half, width), BF16),
            pltpu.VMEM((half, width), BF16),
            pltpu.VMEM((columns, planes, width), BF16),
            pltpu.VMEM((columns, planes, width), BF16),
            pltpu.VMEM((planes, 2, width // 2), BF16),
            pltpu.VMEM((planes, 2, width // 2), BF16),
            dma((3,)),
            dma((2,)),
            dma((2,)),
            dma((2 * columns,)),
            dma((2 * columns,)),
            dma((columns + 1,)),
            dma((columns + 1,)),
        ],
        compiler_params=pltpu.CompilerParams(
            collective_id=0, has_side_effects=True, vmem_limit_bytes=56 * 1024 * 1024
        ),
        cost_estimate=pl.CostEstimate(
            flops=2 * 2 * devices * width * units, bytes_accessed=4 * width * units, transcendentals=0
        ),
    )(tokens, slot_weight.T, w_in, w_out)


def solution(mesh):
    in_specs = (
        P(("rep", "expert"), None, None),
        P("rep", None),
        P(None, "expert"),
        P("expert", None),
    )
    out_specs = P(("rep", "expert"), None, None)
    step = functools.partial(on_device, devices=mesh.shape["expert"], cores_per_chip=CORES)
    return jax.shard_map(step, mesh=mesh, in_specs=in_specs, out_specs=out_specs, check_vma=False)
```

```python
import functools

import jax
import jax.numpy as jnp
from jax import lax
from jax.experimental import pallas as pl
from jax.experimental.pallas import tpu as pltpu
from jax.sharding import PartitionSpec as P

BF16 = jnp.bfloat16
F32 = jnp.float32
CORES = 2
CUTS = (0, 4, 8)


def remote(src, dst, send_sem, recv_sem, target):
    return pltpu.make_async_remote_copy(
        src_ref=src,
        dst_ref=dst,
        send_sem=send_sem,
        recv_sem=recv_sem,
        device_id={"expert": target},
        device_id_type=pl.DeviceIdType.MESH,
    )


def wait_for(rows, sem):
    pltpu.make_async_copy(rows, rows, sem).wait()


def kernel(
    planes,
    side,
    tokens_hbm,
    slot_ref,
    w_in_hbm,
    w_out_hbm,
    combine_ref,
    expert_ref,
    tokens,
    w_in,
    w_out,
    slot_out,
    slots,
    partial,
    scattered,
    expert_out,
    expert_in,
    load_sem,
    send_sem,
    recv_sem,
):
    chunks = list(zip(CUTS, CUTS[1:] + (planes,)))
    count = len(chunks)
    slots, partial, scattered = (
        [ref.at[pl.ds(side * low, side * (high - low))] for low, high in chunks]
        for ref in (slots, partial, scattered)
    )
    me = lax.axis_index("expert")
    place = lax.rem(me, side)
    plane = lax.div(me, side)

    def in_plane(step):
        return lax.rem(plane + step, planes)

    def at_plane(other):
        return other * side + place

    def in_side(step):
        return lax.rem(place + step, side)

    def at_place(other):
        return plane * side + other

    load_tokens = pltpu.make_async_copy(tokens_hbm, tokens, load_sem.at[0])
    load_in = pltpu.make_async_copy(w_in_hbm, w_in, load_sem.at[1])
    load_out = pltpu.make_async_copy(w_out_hbm, w_out, load_sem.at[2])
    load_tokens.start()
    barrier = pltpu.get_barrier_semaphore()
    far_first = sorted(range(1, planes), key=lambda k: -min(k, planes - k))
    peers = [at_plane(in_plane(k)) for k in far_first]
    peers += [at_place(in_side(k)) for k in range(1, side)]
    for peer in peers:
        pl.semaphore_signal(
            barrier, inc=1, device_id={"expert": peer}, device_id_type=pl.DeviceIdType.MESH
        )
    load_in.start()
    load_out.start()

    load_tokens.wait()
    logits = lax.dot_general(
        slot_ref[...], tokens[0], (((1,), (1,)), ((), ())), preferred_element_type=F32
    )
    top = jnp.max(logits, axis=1, keepdims=True)
    weight = jnp.exp(logits - top)
    dispatch = (weight / jnp.sum(weight, axis=1, keepdims=True)).astype(BF16)
    own_slots = jnp.dot(dispatch, tokens[0], preferred_element_type=F32)
    slot_out[...] = own_slots.reshape(slot_out.shape).astype(BF16)

    pl.semaphore_wait(barrier, len(peers))

    def send_slots(landing, sem):
        for k in far_first:
            to = in_plane(k)
            remote(slot_out.at[to], landing, send_sem.at[0], sem, at_plane(to)).start()
        pltpu.make_async_copy(slot_out.at[plane], landing, sem).start()

    for number, (low, high) in enumerate(chunks):

        @pl.when(jnp.logical_and(plane >= low, plane < high))
        def _():
            send_slots(slots[number].at[place * (high - low) + plane - low], recv_sem.at[number])

    top = jnp.max(logits, axis=0, keepdims=True)
    weight = jnp.exp(logits - top)
    combine_ref[...] = (weight / jnp.sum(weight, axis=0, keepdims=True)).astype(BF16)

    def spread(number):
        low, high = chunks[number]
        block = slots[number].at[pl.ds(place * (high - low), high - low)]
        wait_for(block, recv_sem.at[number])
        for k in range(1, side):
            remote(
                block, block, send_sem.at[1 + number], recv_sem.at[count + number], at_place(in_side(k))
            ).start()

    def experts(number):
        low, high = chunks[number]
        rows = high - low
        wait_for(slots[number].at[pl.ds(0, (side - 1) * rows)], recv_sem.at[count + number])
        hidden = jnp.dot(
            slots[number][...].reshape(side * rows, -1), w_in[...], preferred_element_type=F32
        )
        hidden = jax.nn.gelu(hidden).astype(BF16)
        out = jnp.dot(hidden, w_out[...], preferred_element_type=F32)
        partial[number][...] = out.reshape(partial[number].shape).astype(BF16)
        block = scattered[number].at[pl.ds(place * rows, rows)]
        sem = recv_sem.at[2 * count + number]
        for k in range(1, side):
            to = in_side(k)
            remote(
                partial[number].at[pl.ds(to * rows, rows)], block, send_sem.at[1 + count + number], sem, at_place(to)
            ).start()
        pltpu.make_async_copy(partial[number].at[pl.ds(place * rows, rows)], block, sem).start()

    def finish(number):
        low, high = chunks[number]
        rows = high - low
        wait_for(scattered[number], recv_sem.at[2 * count + number])
        total = jnp.zeros((rows * 2, scattered[number].shape[2]), F32)
        for k in range(side):
            part = scattered[number][k * rows : (k + 1) * rows]
            total = total + part.reshape(total.shape).astype(F32)
        expert_out[low:high] = total.astype(BF16).reshape(rows, 2, -1)
        for target in range(low, high):
            own = expert_out.at[target]

            @pl.when(plane == target)
            def _():
                pltpu.make_async_copy(own, expert_in.at[plane], recv_sem.at[3 * count]).start()

            @pl.when(plane != target)
            def _():
                remote(
                    own, expert_in.at[plane], send_sem.at[1 + 2 * count], recv_sem.at[3 * count], at_plane(target)
                ).start()

    spread(0)
    spread(1)
    load_in.wait()
    load_out.wait()
    experts(0)
    spread(2)
    experts(1)
    finish(0)
    experts(2)
    finish(1)
    finish(2)

    wait_for(expert_in, recv_sem.at[3 * count])
    expert_ref[...] = expert_in[...].reshape(expert_ref.shape)

    wait_for(slot_out.at[pl.ds(0, planes - 1)], send_sem.at[0])
    for number, (low, high) in enumerate(chunks):
        others = pl.ds(0, (side - 1) * (high - low))
        wait_for(slots[number].at[others], send_sem.at[1 + number])
        wait_for(partial[number].at[others], send_sem.at[1 + count + number])
    wait_for(expert_out.at[pl.ds(0, planes - 1)], send_sem.at[1 + 2 * count])


def on_device(tokens, slot_weight, w_in, w_out, *, devices):
    images, patches, width = tokens.shape
    experts = slot_weight.shape[1]
    units = w_in.shape[1]
    planes = experts
    side = devices // planes
    dma = pltpu.SemaphoreType.DMA

    def rows(count):
        return pltpu.VMEM((count, 2, width // 2), BF16)

    vmem = pl.BlockSpec(memory_space=pltpu.VMEM)
    hbm = pl.BlockSpec(memory_space=pltpu.HBM)
    combine, expert_out = pl.pallas_call(
        functools.partial(kernel, planes, side),
        out_shape=[
            pltpu.VMEM((experts, patches), BF16),
            pltpu.VMEM((experts, width), BF16),
        ],
        in_specs=[hbm, vmem, hbm, hbm],
        out_specs=[vmem, vmem],
        scratch_shapes=[
            pltpu.VMEM(tokens.shape, BF16),
            pltpu.VMEM((width, units), BF16),
            pltpu.VMEM((units, width), BF16),
            rows(planes),
            rows(devices),
            rows(devices),
            rows(devices),
            rows(planes),
            rows(planes),
            dma((3,)),
            dma((2 + 2 * len(CUTS),)),
            dma((1 + 3 * len(CUTS),)),
        ],
        compiler_params=pltpu.CompilerParams(
            collective_id=0, has_side_effects=True, vmem_limit_bytes=60 * 1024 * 1024
        ),
        cost_estimate=pl.CostEstimate(
            flops=2 * 2 * devices * width * units, bytes_accessed=4 * width * units, transcendentals=0
        ),
    )(tokens, slot_weight.T, w_in, w_out)
    mixed = lax.dot_general(
        combine, expert_out, (((0,), (0,)), ((), ())), preferred_element_type=F32
    )
    return mixed.astype(BF16).reshape(tokens.shape)


def solution(mesh):
    in_specs = (
        P(("rep", "expert"), None, None),
        P("rep", None),
        P(None, "expert"),
        P("expert", None),
    )
    out_specs = P(("rep", "expert"), None, None)
    step = functools.partial(on_device, devices=mesh.shape["expert"])
    return jax.shard_map(step, mesh=mesh, in_specs=in_specs, out_specs=out_specs, check_vma=False)
```

```python
import functools

import jax
import jax.numpy as jnp
from jax import lax
from jax.experimental import pallas as pl
from jax.experimental.pallas import tpu as pltpu
from jax.sharding import PartitionSpec as P

BF16 = jnp.bfloat16
F32 = jnp.float32
CORES = 2
CUTS = (0, 4, 8)
EARLY = CUTS[1]
LOWER = CUTS[2]
HOP = 4
VIA = (7, 8, 9)
LAST = LOWER + HOP


def remote(src, dst, send_sem, recv_sem, target):
    return pltpu.make_async_remote_copy(
        src_ref=src,
        dst_ref=dst,
        send_sem=send_sem,
        recv_sem=recv_sem,
        device_id={"expert": target},
        device_id_type=pl.DeviceIdType.MESH,
    )


def wait_for(rows, sem):
    pltpu.make_async_copy(rows, rows, sem).wait()


def kernel(
    planes,
    side,
    tokens_hbm,
    slot_ref,
    w_in_hbm,
    w_out_hbm,
    combine_ref,
    expert_ref,
    tokens,
    w_in,
    w_out,
    slot_out,
    relay,
    relay_back,
    slots,
    partial,
    scattered,
    expert_out,
    expert_in,
    load_sem,
    send_sem,
    recv_sem,
    ready_sem,
    go_sem,
    relay_sem,
):
    chunks = list(zip(CUTS, CUTS[1:] + (planes,)))
    count = len(chunks)
    slots, partial, scattered = (
        [ref.at[pl.ds(side * low, side * (high - low))] for low, high in chunks]
        for ref in (slots, partial, scattered)
    )
    me = lax.axis_index("expert")
    place = lax.rem(me, side)
    plane = lax.div(me, side)

    is_early = plane < EARLY
    is_high = plane >= LOWER
    is_middle = jnp.logical_and(plane >= EARLY, plane < LOWER)
    is_last = plane >= LAST

    def at_plane(other):
        return other * side + place

    def in_side(step):
        return lax.rem(place + step, side)

    def at_place(other):
        return plane * side + other

    def tell(sem, target):
        pl.semaphore_signal(
            sem, inc=1, device_id={"expert": target}, device_id_type=pl.DeviceIdType.MESH
        )

    load_tokens = pltpu.make_async_copy(tokens_hbm, tokens, load_sem.at[0])
    load_in = pltpu.make_async_copy(w_in_hbm, w_in, load_sem.at[1])
    load_out = pltpu.make_async_copy(w_out_hbm, w_out, load_sem.at[2])
    load_tokens.start()
    barrier = pltpu.get_barrier_semaphore()

    @pl.when(is_last)
    def _():
        pl.semaphore_wait(barrier, EARLY)

    @pl.when(jnp.logical_and(is_high, jnp.logical_not(is_last)))
    def _():
        pl.semaphore_wait(barrier, LOWER)

    @pl.when(jnp.logical_not(is_high))
    def _():
        for other in range(1, LAST):

            @pl.when(plane < other)
            def _():
                tell(barrier, at_plane(other))

        @pl.when(is_early)
        def _():
            for other in range(LAST, planes):
                tell(barrier, at_plane(other))

        for k in range(1, side):
            tell(barrier, at_place(in_side(k)))
        pl.semaphore_wait(barrier, plane + (side - 1))

    for other in range(LOWER):
        answers = plane > other
        if other >= EARLY:
            answers = jnp.logical_and(answers, jnp.logical_not(is_last))

        @pl.when(answers)
        def _():
            tell(ready_sem.at[plane], at_plane(other))

    load_in.start()
    load_out.start()

    load_tokens.wait()
    logits = lax.dot_general(
        slot_ref[...], tokens[0], (((1,), (1,)), ((), ())), preferred_element_type=F32
    )
    top = jnp.max(logits, axis=1, keepdims=True)
    weight = jnp.exp(logits - top)
    dispatch = (weight / jnp.sum(weight, axis=1, keepdims=True)).astype(BF16)
    own_slots = jnp.dot(dispatch, tokens[0], preferred_element_type=F32)
    slot_out[...] = own_slots.reshape(slot_out.shape).astype(BF16)

    def send_to(e, landing, sem):
        remote(slot_out.at[e], landing, send_sem.at[0], sem, at_plane(e)).start()

    def keep(landing, sem):
        pltpu.make_async_copy(slot_out.at[plane], landing, sem).start()

    @pl.when(is_early)
    def _():
        landing, sem = slots[0].at[place * EARLY + plane], recv_sem.at[0]
        keep(landing, sem)

        def send(e):
            by_way = jnp.logical_and(e >= plane + VIA[0], e <= plane + VIA[-1])
            by_way = jnp.logical_and(by_way, e < LAST)

            @pl.when(plane > e)
            def _():
                send_to(e, landing, sem)

            @pl.when(jnp.logical_and(plane < e, jnp.logical_not(by_way)))
            def _():
                pl.semaphore_wait(ready_sem.at[e], 1)
                send_to(e, landing, sem)

            @pl.when(plane + HOP == e)
            def _():
                remote(
                    slot_out.at[pl.ds(plane + VIA[0], len(VIA))], relay, relay_sem.at[0], relay_sem.at[1], at_plane(e)
                ).start()

        for e in (*range(LOWER), *reversed(range(LAST, planes)), *range(LOWER, LAST)):
            send(e)
        for offset in VIA:

            @pl.when(plane + offset < LAST)
            def _():
                pl.semaphore_wait(ready_sem.at[plane + offset], 1)

        @pl.when(plane == 0)
        def _():
            for k in range(1, side):
                tell(go_sem.at[1], at_place(in_side(k)))
            for other in range(LOWER, planes):
                tell(go_sem.at[2], at_plane(other))

        wait_for(relay_back, relay_sem.at[4])
        for number in range(planes - LAST):
            e = LAST + number
            remote(
                relay_back.at[number],
                slots[1].at[place * (LOWER - EARLY) + plane],
                relay_sem.at[5],
                recv_sem.at[1],
                at_plane(e),
            ).start()

        @pl.when(plane == 0)
        def _():
            pl.semaphore_wait(go_sem.at[1], side - 1)
            for other in range(LAST, planes):
                tell(go_sem.at[0], at_plane(other))

    @pl.when(is_middle)
    def _():
        landing, sem = slots[1].at[place * (LOWER - EARLY) + plane - EARLY], recv_sem.at[1]
        remote(
            slot_out.at[pl.ds(LAST, planes - LAST)], relay_back, relay_sem.at[3], relay_sem.at[4], at_plane(plane - HOP)
        ).start()
        keep(landing, sem)

        def send(e):
            @pl.when(plane > e)
            def _():
                send_to(e, landing, sem)

            @pl.when(plane < e)
            def _():
                pl.semaphore_wait(ready_sem.at[e], 1)
                send_to(e, landing, sem)

        def forward():
            wait_for(relay, relay_sem.at[1])
            for number, offset in enumerate(VIA):
                e = plane + offset - HOP

                @pl.when(e < LAST)
                def _():
                    remote(
                        relay.at[number],
                        slots[0].at[place * EARLY + plane - HOP],
                        relay_sem.at[2],
                        recv_sem.at[0],
                        at_plane(e),
                    ).start()

        beyond = plane + VIA[-1] - HOP + 1
        for e in range(LOWER):
            send(e)
        for e in range(LOWER, LAST):
            pl.when(beyond == e)(forward)
            send(e)

        @pl.when(plane == LOWER - 1)
        def _():
            for k in range(1, side):
                tell(go_sem.at[1], at_place(in_side(k)))
            pl.semaphore_wait(go_sem.at[1], side - 1)
            for other in range(LOWER, LAST):
                tell(go_sem.at[0], at_plane(other))

        pl.when(beyond >= LAST)(forward)

    landing_high = slots[2].at[place * (planes - LOWER) + plane - LOWER]

    @pl.when(is_high)
    def _():
        keep(landing_high, recv_sem.at[2])
        for e in range(EARLY):
            send_to(e, landing_high, recv_sem.at[2])

    def send_next():
        for e in range(EARLY, LOWER):
            send_to(e, landing_high, recv_sem.at[2])

    pl.when(jnp.logical_and(is_high, jnp.logical_not(is_last)))(send_next)

    def send_high():
        pl.semaphore_wait(go_sem.at[2], 1)
        for e in range(LOWER, planes):

            @pl.when(plane != e)
            def _():
                send_to(e, landing_high, recv_sem.at[2])

    top = jnp.max(logits, axis=0, keepdims=True)
    weight = jnp.exp(logits - top)
    combine_ref[...] = (weight / jnp.sum(weight, axis=0, keepdims=True)).astype(BF16)

    def spread(number):
        low, high = chunks[number]
        block = slots[number].at[pl.ds(place * (high - low), high - low)]
        wait_for(block, recv_sem.at[number])
        for k in range(1, side):
            remote(
                block, block, send_sem.at[1 + number], recv_sem.at[count + number], at_place(in_side(k))
            ).start()

    def experts(number):
        low, high = chunks[number]
        rows = high - low
        wait_for(slots[number].at[pl.ds(0, (side - 1) * rows)], recv_sem.at[count + number])
        block = slots[number][...]
        hidden = jnp.dot(
            block.reshape(side * rows, -1), w_in[...], preferred_element_type=F32
        )
        hidden = jax.nn.gelu(hidden).astype(BF16)
        out = jnp.dot(hidden, w_out[...], preferred_element_type=F32)
        partial[number][...] = out.reshape(partial[number].shape).astype(BF16)
        block = scattered[number].at[pl.ds(place * rows, rows)]
        sem = recv_sem.at[2 * count + number]
        for k in range(1, side):
            to = in_side(k)
            remote(
                partial[number].at[pl.ds(to * rows, rows)], block, send_sem.at[1 + count + number], sem, at_place(to)
            ).start()
        pltpu.make_async_copy(partial[number].at[pl.ds(place * rows, rows)], block, sem).start()

    def finish(number):
        low, high = chunks[number]
        rows = high - low
        wait_for(scattered[number], recv_sem.at[2 * count + number])
        total = jnp.zeros((rows * 2, scattered[number].shape[2]), F32)
        for k in range(side):
            part = scattered[number][k * rows : (k + 1) * rows]
            total = total + part.reshape(total.shape).astype(F32)
        expert_out[low:high] = total.astype(BF16).reshape(rows, 2, -1)
        for target in range(low, high):
            own = expert_out.at[target]

            @pl.when(plane == target)
            def _():
                pltpu.make_async_copy(own, expert_in.at[plane], recv_sem.at[3 * count]).start()

            @pl.when(plane != target)
            def _():
                remote(
                    own, expert_in.at[plane], send_sem.at[1 + 2 * count], recv_sem.at[3 * count], at_plane(target)
                ).start()

    @pl.when(is_high)
    def _():
        pl.semaphore_wait(go_sem.at[0], 1)

    spread(0)
    @pl.when(is_high)
    def _():
        send_high()

    spread(1)
    pl.when(is_last)(send_next)
    load_in.wait()
    load_out.wait()
    experts(0)
    spread(2)
    experts(1)
    finish(0)
    experts(2)
    finish(1)
    finish(2)

    wait_for(expert_in, recv_sem.at[3 * count])
    expert_ref[...] = expert_in[...].reshape(expert_ref.shape)

    @pl.when(is_early)
    def _():
        wait_for(relay, relay_sem.at[0])
        wait_for(relay_back, relay_sem.at[5])

    @pl.when(plane < EARLY - 1)
    def _():
        wait_for(slot_out.at[pl.ds(0, planes - 1 - len(VIA))], send_sem.at[0])

    @pl.when(plane == EARLY - 1)
    def _():
        wait_for(slot_out.at[pl.ds(0, planes - len(VIA))], send_sem.at[0])

    @pl.when(is_middle)
    def _():
        wait_for(slot_out.at[pl.ds(0, LAST - 1)], send_sem.at[0])
        wait_for(relay_back, relay_sem.at[3])

    @pl.when(jnp.logical_and(is_middle, plane < LOWER - 1))
    def _():
        wait_for(relay, relay_sem.at[2])

    @pl.when(plane == LOWER - 1)
    def _():
        wait_for(relay.at[pl.ds(0, len(VIA) - 1)], relay_sem.at[2])

    @pl.when(is_high)
    def _():
        wait_for(slot_out.at[pl.ds(0, planes - 1)], send_sem.at[0])

    for number, (low, high) in enumerate(chunks):
        others = pl.ds(0, (side - 1) * (high - low))
        wait_for(slots[number].at[others], send_sem.at[1 + number])
        wait_for(partial[number].at[others], send_sem.at[1 + count + number])
    wait_for(expert_out.at[pl.ds(0, planes - 1)], send_sem.at[1 + 2 * count])


def on_device(tokens, slot_weight, w_in, w_out, *, devices):
    images, patches, width = tokens.shape
    experts = slot_weight.shape[1]
    units = w_in.shape[1]
    planes = experts
    side = devices // planes
    dma = pltpu.SemaphoreType.DMA

    def rows(count):
        return pltpu.VMEM((count, 2, width // 2), BF16)

    vmem = pl.BlockSpec(memory_space=pltpu.VMEM)
    hbm = pl.BlockSpec(memory_space=pltpu.HBM)
    combine, expert_out = pl.pallas_call(
        functools.partial(kernel, planes, side),
        out_shape=[
            pltpu.VMEM((experts, patches), BF16),
            pltpu.VMEM((experts, width), BF16),
        ],
        in_specs=[hbm, vmem, hbm, hbm],
        out_specs=[vmem, vmem],
        scratch_shapes=[
            pltpu.VMEM(tokens.shape, BF16),
            pltpu.VMEM((width, units), BF16),
            pltpu.VMEM((units, width), BF16),
            rows(planes),
            rows(len(VIA)),
            rows(HOP),
            rows(devices),
            rows(devices),
            rows(devices),
            rows(planes),
            rows(planes),
            dma((3,)),
            dma((2 + 2 * len(CUTS),)),
            dma((1 + 3 * len(CUTS),)),
            pltpu.SemaphoreType.REGULAR((planes,)),
            pltpu.SemaphoreType.REGULAR((3,)),
            dma((6,)),
        ],
        compiler_params=pltpu.CompilerParams(
            collective_id=0, has_side_effects=True, vmem_limit_bytes=60 * 1024 * 1024
        ),
        cost_estimate=pl.CostEstimate(
            flops=2 * 2 * devices * width * units, bytes_accessed=4 * width * units, transcendentals=0
        ),
    )(tokens, slot_weight.T, w_in, w_out)
    mixed = lax.dot_general(
        combine, expert_out, (((0,), (0,)), ((), ())), preferred_element_type=F32
    )
    return mixed.astype(BF16).reshape(tokens.shape)


def solution(mesh):
    in_specs = (
        P(("rep", "expert"), None, None),
        P("rep", None),
        P(None, "expert"),
        P("expert", None),
    )
    out_specs = P(("rep", "expert"), None, None)
    step = functools.partial(on_device, devices=mesh.shape["expert"])
    return jax.shard_map(step, mesh=mesh, in_specs=in_specs, out_specs=out_specs, check_vma=False)
```

```python
import functools

import jax
import jax.numpy as jnp
from jax import lax
from jax.experimental import pallas as pl
from jax.experimental.pallas import tpu as pltpu
from jax.sharding import PartitionSpec as P

BF16 = jnp.bfloat16
F32 = jnp.float32
CORES = 2
CUTS = (0, 2, 8)
SIDE_ORDER = ((2, 0), (2, 1), (1, 0), (3, 0), (1, 1), (3, 1), (0, 1))


def remote(src, dst, send_sem, recv_sem, target):
    return pltpu.make_async_remote_copy(
        src_ref=src,
        dst_ref=dst,
        send_sem=send_sem,
        recv_sem=recv_sem,
        device_id={"expert": target},
        device_id_type=pl.DeviceIdType.MESH,
    )


def wait_for(rows, sem):
    pltpu.make_async_copy(rows, rows, sem).wait()


def kernel(
    planes,
    side,
    tokens_hbm,
    slot_ref,
    w_in_hbm,
    w_out_hbm,
    combine_ref,
    expert_ref,
    tokens,
    w_in,
    w_out,
    slot_out,
    slots,
    partial,
    scattered,
    expert_out,
    expert_in,
    load_sem,
    send_sem,
    recv_sem,
):
    chunks = list(zip(CUTS, CUTS[1:] + (planes,)))
    count = len(chunks)
    slots, partial, scattered = (
        [ref.at[pl.ds(side * low, side * (high - low))] for low, high in chunks]
        for ref in (slots, partial, scattered)
    )
    me = lax.axis_index("expert")
    place = lax.rem(me, side)
    plane = lax.div(me, side)

    def in_plane(step):
        return lax.rem(plane + step, planes)

    def at_plane(other):
        return other * side + place

    core = lax.rem(place, CORES)
    columns = side // CORES

    def in_side(step):
        column, other = SIDE_ORDER[step - 1]
        column = lax.rem(lax.div(place, CORES) + column, columns)
        return column * CORES + (1 - core if other else core)

    def at_place(other):
        return plane * side + other

    load_tokens = pltpu.make_async_copy(tokens_hbm, tokens, load_sem.at[0])
    load_in = pltpu.make_async_copy(w_in_hbm, w_in, load_sem.at[1])
    load_out = pltpu.make_async_copy(w_out_hbm, w_out, load_sem.at[2])
    load_tokens.start()
    barrier = pltpu.get_barrier_semaphore()
    far_first = sorted(range(1, planes), key=lambda k: -min(k, planes - k))
    peers = [at_plane(in_plane(k)) for k in far_first]
    peers += [at_place(in_side(k)) for k in range(1, side)]
    for peer in peers:
        pl.semaphore_signal(
            barrier, inc=1, device_id={"expert": peer}, device_id_type=pl.DeviceIdType.MESH
        )
    load_in.start()
    load_out.start()

    load_tokens.wait()
    logits = lax.dot_general(
        slot_ref[...], tokens[0], (((1,), (1,)), ((), ())), preferred_element_type=F32
    )
    top = jnp.max(logits, axis=1, keepdims=True)
    weight = jnp.exp(logits - top)
    dispatch = (weight / jnp.sum(weight, axis=1, keepdims=True)).astype(BF16)
    own_slots = jnp.dot(dispatch, tokens[0], preferred_element_type=F32)
    slot_out[...] = own_slots.reshape(slot_out.shape).astype(BF16)

    pl.semaphore_wait(barrier, len(peers))

    def send_slots(landing, sem):
        for k in far_first:
            to = in_plane(k)
            remote(slot_out.at[to], landing, send_sem.at[0], sem, at_plane(to)).start()
        pltpu.make_async_copy(slot_out.at[plane], landing, sem).start()

    for number, (low, high) in enumerate(chunks):

        @pl.when(jnp.logical_and(plane >= low, plane < high))
        def _():
            send_slots(slots[number].at[place * (high - low) + plane - low], recv_sem.at[number])

    top = jnp.max(logits, axis=0, keepdims=True)
    weight = jnp.exp(logits - top)
    combine_ref[...] = (weight / jnp.sum(weight, axis=0, keepdims=True)).astype(BF16)

    def spread(number):
        low, high = chunks[number]
        block = slots[number].at[pl.ds(place * (high - low), high - low)]
        wait_for(block, recv_sem.at[number])
        for k in range(1, side):
            remote(
                block, block, send_sem.at[1 + number], recv_sem.at[count + number], at_place(in_side(k))
            ).start()

    def experts(number):
        low, high = chunks[number]
        rows = high - low
        wait_for(slots[number].at[pl.ds(0, (side - 1) * rows)], recv_sem.at[count + number])
        hidden = jnp.dot(
            slots[number][...].reshape(side * rows, -1), w_in[...], preferred_element_type=F32
        )
        hidden = jax.nn.gelu(hidden).astype(BF16)
        out = jnp.dot(hidden, w_out[...], preferred_element_type=F32)
        partial[number][...] = out.reshape(partial[number].shape).astype(BF16)
        block = scattered[number].at[pl.ds(place * rows, rows)]
        sem = recv_sem.at[2 * count + number]
        for k in range(1, side):
            to = in_side(k)
            remote(
                partial[number].at[pl.ds(to * rows, rows)], block, send_sem.at[1 + count + number], sem, at_place(to)
            ).start()
        pltpu.make_async_copy(partial[number].at[pl.ds(place * rows, rows)], block, sem).start()

    def finish(number):
        low, high = chunks[number]
        rows = high - low
        wait_for(scattered[number], recv_sem.at[2 * count + number])
        total = jnp.zeros((rows * 2, scattered[number].shape[2]), F32)
        for k in range(side):
            part = scattered[number][k * rows : (k + 1) * rows]
            total = total + part.reshape(total.shape).astype(F32)
        expert_out[low:high] = total.astype(BF16).reshape(rows, 2, -1)
        for target in range(low, high):
            own = expert_out.at[target]

            @pl.when(plane == target)
            def _():
                pltpu.make_async_copy(own, expert_in.at[plane], recv_sem.at[3 * count]).start()

            @pl.when(plane != target)
            def _():
                remote(
                    own, expert_in.at[plane], send_sem.at[1 + 2 * count], recv_sem.at[3 * count], at_plane(target)
                ).start()

    spread(0)
    spread(1)
    spread(2)
    load_in.wait()
    load_out.wait()
    experts(0)
    experts(1)
    finish(0)
    experts(2)
    finish(1)
    finish(2)

    wait_for(expert_in, recv_sem.at[3 * count])
    expert_ref[...] = expert_in[...].reshape(expert_ref.shape)

    wait_for(slot_out.at[pl.ds(0, planes - 1)], send_sem.at[0])
    for number, (low, high) in enumerate(chunks):
        others = pl.ds(0, (side - 1) * (high - low))
        wait_for(slots[number].at[others], send_sem.at[1 + number])
        wait_for(partial[number].at[others], send_sem.at[1 + count + number])
    wait_for(expert_out.at[pl.ds(0, planes - 1)], send_sem.at[1 + 2 * count])


def on_device(tokens, slot_weight, w_in, w_out, *, devices):
    images, patches, width = tokens.shape
    experts = slot_weight.shape[1]
    units = w_in.shape[1]
    planes = experts
    side = devices // planes
    dma = pltpu.SemaphoreType.DMA

    def rows(count):
        return pltpu.VMEM((count, 2, width // 2), BF16)

    vmem = pl.BlockSpec(memory_space=pltpu.VMEM)
    hbm = pl.BlockSpec(memory_space=pltpu.HBM)
    combine, expert_out = pl.pallas_call(
        functools.partial(kernel, planes, side),
        out_shape=[
            pltpu.VMEM((experts, patches), BF16),
            pltpu.VMEM((experts, width), BF16),
        ],
        in_specs=[hbm, vmem, hbm, hbm],
        out_specs=[vmem, vmem],
        scratch_shapes=[
            pltpu.VMEM(tokens.shape, BF16),
            pltpu.VMEM((width, units), BF16),
            pltpu.VMEM((units, width), BF16),
            rows(planes),
            rows(devices),
            rows(devices),
            rows(devices),
            rows(planes),
            rows(planes),
            dma((3,)),
            dma((2 + 2 * len(CUTS),)),
            dma((1 + 3 * len(CUTS),)),
        ],
        compiler_params=pltpu.CompilerParams(
            collective_id=0, has_side_effects=True, vmem_limit_bytes=60 * 1024 * 1024
        ),
        cost_estimate=pl.CostEstimate(
            flops=2 * 2 * devices * width * units, bytes_accessed=4 * width * units, transcendentals=0
        ),
    )(tokens, slot_weight.T, w_in, w_out)
    mixed = lax.dot_general(
        combine, expert_out, (((0,), (0,)), ((), ())), preferred_element_type=F32
    )
    return mixed.astype(BF16).reshape(tokens.shape)


def solution(mesh):
    in_specs = (
        P(("rep", "expert"), None, None),
        P("rep", None),
        P(None, "expert"),
        P("expert", None),
    )
    out_specs = P(("rep", "expert"), None, None)
    step = functools.partial(on_device, devices=mesh.shape["expert"])
    return jax.shard_map(step, mesh=mesh, in_specs=in_specs, out_specs=out_specs, check_vma=False)
```

```python
import functools

import jax
import jax.numpy as jnp
from jax import lax
from jax.experimental import pallas as pl
from jax.experimental.pallas import tpu as pltpu
from jax.sharding import PartitionSpec as P

BF16 = jnp.bfloat16
F32 = jnp.float32
CORES = 2
CUTS = (0, 2, 4)
SIDE_ORDER = ((2, 0), (2, 1), (1, 0), (3, 0), (1, 1), (3, 1), (0, 1))


def remote(src, dst, send_sem, recv_sem, target):
    return pltpu.make_async_remote_copy(
        src_ref=src,
        dst_ref=dst,
        send_sem=send_sem,
        recv_sem=recv_sem,
        device_id={"expert": target},
        device_id_type=pl.DeviceIdType.MESH,
    )


def wait_for(rows, sem):
    pltpu.make_async_copy(rows, rows, sem).wait()


def kernel(
    planes,
    side,
    tokens_hbm,
    slot_ref,
    w_in_hbm,
    w_out_hbm,
    combine_ref,
    expert_ref,
    tokens,
    w_in,
    w_out,
    slot_out,
    slots,
    partial,
    scattered,
    direct,
    expert_out,
    expert_in,
    load_sem,
    send_sem,
    recv_sem,
):
    chunks = list(zip(CUTS, CUTS[1:] + (planes,)))
    count = len(chunks)
    slots, partial, scattered = (
        [ref.at[pl.ds(side * low, side * (high - low))] for low, high in chunks]
        for ref in (slots, partial, scattered)
    )
    me = lax.axis_index("expert")
    place = lax.rem(me, side)
    plane = lax.div(me, side)

    def in_plane(step):
        return lax.rem(plane + step, planes)

    def at_plane(other):
        return other * side + place

    core = lax.rem(place, CORES)
    columns = side // CORES

    def in_side(step):
        column, other = SIDE_ORDER[step - 1]
        column = lax.rem(lax.div(place, CORES) + column, columns)
        return column * CORES + (1 - core if other else core)

    def at_place(other):
        return plane * side + other

    load_tokens = pltpu.make_async_copy(tokens_hbm, tokens, load_sem.at[0])
    load_in = pltpu.make_async_copy(w_in_hbm, w_in, load_sem.at[1])
    load_out = pltpu.make_async_copy(w_out_hbm, w_out, load_sem.at[2])
    load_tokens.start()
    barrier = pltpu.get_barrier_semaphore()
    far_first = sorted(range(1, planes), key=lambda k: -min(k, planes - k))
    peers = [at_plane(in_plane(k)) for k in far_first]
    peers += [at_place(in_side(k)) for k in range(1, side)]
    for peer in peers:
        pl.semaphore_signal(
            barrier, inc=1, device_id={"expert": peer}, device_id_type=pl.DeviceIdType.MESH
        )
    load_in.start()
    load_out.start()

    load_tokens.wait()
    logits = lax.dot_general(
        slot_ref[...], tokens[0], (((1,), (1,)), ((), ())), preferred_element_type=F32
    )
    top = jnp.max(logits, axis=1, keepdims=True)
    weight = jnp.exp(logits - top)
    dispatch = (weight / jnp.sum(weight, axis=1, keepdims=True)).astype(BF16)
    own_slots = jnp.dot(dispatch, tokens[0], preferred_element_type=F32)
    slot_out[...] = own_slots.reshape(slot_out.shape).astype(BF16)

    pl.semaphore_wait(barrier, len(peers))

    def send_slots(landing, sem):
        for k in far_first:
            to = in_plane(k)
            remote(slot_out.at[to], landing, send_sem.at[0], sem, at_plane(to)).start()
        pltpu.make_async_copy(slot_out.at[plane], landing, sem).start()

    for number, (low, high) in enumerate(chunks):

        @pl.when(jnp.logical_and(plane >= low, plane < high))
        def _():
            send_slots(slots[number].at[place * (high - low) + plane - low], recv_sem.at[number])

    top = jnp.max(logits, axis=0, keepdims=True)
    weight = jnp.exp(logits - top)
    combine = (weight / jnp.sum(weight, axis=0, keepdims=True)).astype(BF16)
    is_first = plane < CUTS[1]

    @pl.when(is_first)
    def _():
        combine_ref[...] = jnp.broadcast_to(
            combine[:, None, :], (planes, side, combine.shape[1])
        ).reshape(combine_ref.shape)

    @pl.when(jnp.logical_not(is_first))
    def _():
        combine_ref[:planes] = combine
        combine_ref[planes:] = jnp.zeros((planes * (side - 1), combine.shape[1]), BF16)
        expert_ref[planes:] = jnp.zeros((planes * (side - 1), expert_ref.shape[1]), BF16)


    def spread(number):
        low, high = chunks[number]
        block = slots[number].at[pl.ds(place * (high - low), high - low)]
        wait_for(block, recv_sem.at[number])
        for k in range(1, side):
            remote(
                block, block, send_sem.at[1 + number], recv_sem.at[count + number], at_place(in_side(k))
            ).start()

    def send_direct():
        here, sem = direct.at[me], recv_sem.at[2 * count]
        for target in range(CUTS[1]):
            for k in range(1, side):
                to = in_side(k)
                own = partial[0].at[to * CUTS[1] + target]
                remote(own, here, send_sem.at[1 + count], sem, target * side + to).start()
            own = partial[0].at[place * CUTS[1] + target]

            @pl.when(plane == target)
            def _():
                pltpu.make_async_copy(own, here, sem).start()

            @pl.when(plane != target)
            def _():
                remote(own, here, send_sem.at[1 + count], sem, target * side + place).start()

    def experts(number):
        low, high = chunks[number]
        rows = high - low
        wait_for(slots[number].at[pl.ds(0, (side - 1) * rows)], recv_sem.at[count + number])
        hidden = jnp.dot(
            slots[number][...].reshape(side * rows, -1), w_in[...], preferred_element_type=F32
        )
        hidden = jax.nn.gelu(hidden).astype(BF16)
        out = jnp.dot(hidden, w_out[...], preferred_element_type=F32)
        partial[number][...] = out.reshape(partial[number].shape).astype(BF16)
        if number == 0:
            return send_direct()
        block = scattered[number].at[pl.ds(place * rows, rows)]
        sem = recv_sem.at[2 * count + number]
        for k in range(1, side):
            to = in_side(k)
            remote(
                partial[number].at[pl.ds(to * rows, rows)], block, send_sem.at[1 + count + number], sem, at_place(to)
            ).start()
        pltpu.make_async_copy(partial[number].at[pl.ds(place * rows, rows)], block, sem).start()

    def finish(number):
        low, high = chunks[number]
        rows = high - low
        wait_for(scattered[number], recv_sem.at[2 * count + number])
        total = jnp.zeros((rows * 2, scattered[number].shape[2]), F32)
        for k in range(side):
            part = scattered[number][k * rows : (k + 1) * rows]
            total = total + part.reshape(total.shape).astype(F32)
        expert_out[low:high] = total.astype(BF16).reshape(rows, 2, -1)
        for target in range(low, high):
            own = expert_out.at[target]

            @pl.when(plane == target)
            def _():
                pltpu.make_async_copy(own, expert_in.at[plane], recv_sem.at[3 * count]).start()

            @pl.when(plane != target)
            def _():
                remote(
                    own, expert_in.at[plane], send_sem.at[1 + 2 * count], recv_sem.at[3 * count], at_plane(target)
                ).start()

    spread(0)
    spread(1)
    spread(2)
    load_in.wait()
    load_out.wait()
    experts(0)
    experts(1)
    experts(2)
    finish(1)
    finish(2)

    @pl.when(is_first)
    def _():
        wait_for(direct, recv_sem.at[2 * count])
        expert_ref[...] = direct[...].reshape(expert_ref.shape)

    @pl.when(jnp.logical_not(is_first))
    def _():
        wait_for(expert_in, recv_sem.at[3 * count])
        expert_ref[:planes] = expert_in[...].reshape(planes, -1)

    wait_for(slot_out.at[pl.ds(0, planes - 1)], send_sem.at[0])
    for number, (low, high) in enumerate(chunks):
        others = pl.ds(0, (side - 1) * (high - low))
        wait_for(slots[number].at[others], send_sem.at[1 + number])
        if number > 0:
            wait_for(partial[number].at[others], send_sem.at[1 + count + number])

    @pl.when(is_first)
    def _():
        wait_for(partial[0].at[pl.ds(0, side * CUTS[1] - 1)], send_sem.at[1 + count])
        wait_for(expert_out.at[pl.ds(0, planes - CUTS[1])], send_sem.at[1 + 2 * count])

    @pl.when(jnp.logical_not(is_first))
    def _():
        wait_for(partial[0], send_sem.at[1 + count])
        wait_for(expert_out.at[pl.ds(0, planes - CUTS[1] - 1)], send_sem.at[1 + 2 * count])


def on_device(tokens, slot_weight, w_in, w_out, *, devices):
    images, patches, width = tokens.shape
    experts = slot_weight.shape[1]
    units = w_in.shape[1]
    planes = experts
    side = devices // planes
    dma = pltpu.SemaphoreType.DMA

    def rows(count):
        return pltpu.VMEM((count, 2, width // 2), BF16)

    vmem = pl.BlockSpec(memory_space=pltpu.VMEM)
    hbm = pl.BlockSpec(memory_space=pltpu.HBM)
    combine, expert_out = pl.pallas_call(
        functools.partial(kernel, planes, side),
        out_shape=[
            pltpu.VMEM((devices, patches), BF16),
            pltpu.VMEM((devices, width), BF16),
        ],
        in_specs=[hbm, vmem, hbm, hbm],
        out_specs=[vmem, vmem],
        scratch_shapes=[
            pltpu.VMEM(tokens.shape, BF16),
            pltpu.VMEM((width, units), BF16),
            pltpu.VMEM((units, width), BF16),
            rows(planes),
            rows(devices),
            rows(devices),
            rows(devices),
            rows(devices),
            rows(planes),
            rows(planes),
            dma((3,)),
            dma((2 + 2 * len(CUTS),)),
            dma((1 + 3 * len(CUTS),)),
        ],
        compiler_params=pltpu.CompilerParams(
            collective_id=0, has_side_effects=True, vmem_limit_bytes=60 * 1024 * 1024
        ),
        cost_estimate=pl.CostEstimate(
            flops=2 * 2 * devices * width * units, bytes_accessed=4 * width * units, transcendentals=0
        ),
    )(tokens, slot_weight.T, w_in, w_out)
    mixed = lax.dot_general(
        combine, expert_out, (((0,), (0,)), ((), ())), preferred_element_type=F32
    )
    return mixed.astype(BF16).reshape(tokens.shape)


def solution(mesh):
    in_specs = (
        P(("rep", "expert"), None, None),
        P("rep", None),
        P(None, "expert"),
        P("expert", None),
    )
    out_specs = P(("rep", "expert"), None, None)
    step = functools.partial(on_device, devices=mesh.shape["expert"])
    return jax.shard_map(step, mesh=mesh, in_specs=in_specs, out_specs=out_specs, check_vma=False)
```

```python
import functools

import jax
import jax.numpy as jnp
from jax import lax
from jax.experimental import pallas as pl
from jax.experimental.pallas import tpu as pltpu
from jax.sharding import PartitionSpec as P

BF16 = jnp.bfloat16
F32 = jnp.float32
CORES = 2
CUTS = (0, 2, 4)
SIDE_ORDER = ((2, 0), (2, 1), (1, 0), (3, 0), (1, 1), (3, 1), (0, 1))


def remote(src, dst, send_sem, recv_sem, target):
    return pltpu.make_async_remote_copy(
        src_ref=src,
        dst_ref=dst,
        send_sem=send_sem,
        recv_sem=recv_sem,
        device_id={"expert": target},
        device_id_type=pl.DeviceIdType.MESH,
    )


def wait_for(rows, sem):
    pltpu.make_async_copy(rows, rows, sem).wait()


def kernel(
    planes,
    side,
    tokens_hbm,
    slot_hbm,
    w_in_hbm,
    w_out_hbm,
    combine_ref,
    expert_ref,
    slot_weight,
    tokens,
    w_in,
    w_out,
    slot_out,
    slots,
    partial,
    scattered,
    direct,
    expert_out,
    expert_in,
    load_sem,
    send_sem,
    recv_sem,
):
    chunks = list(zip(CUTS, CUTS[1:] + (planes,)))
    count = len(chunks)
    slots, partial, scattered = (
        [ref.at[pl.ds(side * low, side * (high - low))] for low, high in chunks]
        for ref in (slots, partial, scattered)
    )
    me = lax.axis_index("expert")
    place = lax.rem(me, side)
    plane = lax.div(me, side)

    def in_plane(step):
        return lax.rem(plane + step, planes)

    def at_plane(other):
        return other * side + place

    core = lax.rem(place, CORES)
    columns = side // CORES

    def in_side(step):
        column, other = SIDE_ORDER[step - 1]
        column = lax.rem(lax.div(place, CORES) + column, columns)
        return column * CORES + (1 - core if other else core)

    def at_place(other):
        return plane * side + other

    load_tokens = pltpu.make_async_copy(tokens_hbm, tokens, load_sem.at[0])
    load_slot = pltpu.make_async_copy(slot_hbm, slot_weight, load_sem.at[3])
    load_in = pltpu.make_async_copy(w_in_hbm, w_in, load_sem.at[1])
    load_out = pltpu.make_async_copy(w_out_hbm, w_out, load_sem.at[2])
    barrier = pltpu.get_barrier_semaphore()
    far_first = sorted(range(1, planes), key=lambda k: -min(k, planes - k))
    peers = [at_plane(in_plane(k)) for k in far_first]
    peers += [at_place(in_side(k)) for k in range(1, side)]
    for peer in peers:
        pl.semaphore_signal(
            barrier, inc=1, device_id={"expert": peer}, device_id_type=pl.DeviceIdType.MESH
        )
    load_slot.start()
    load_tokens.start()
    load_in.start()
    load_out.start()

    load_slot.wait()
    load_tokens.wait()
    logits = lax.dot_general(
        slot_weight[...], tokens[0], (((1,), (1,)), ((), ())), preferred_element_type=F32
    )
    top = jnp.max(logits, axis=1, keepdims=True)
    weight = jnp.exp(logits - top)
    dispatch = (weight / jnp.sum(weight, axis=1, keepdims=True)).astype(BF16)
    own_slots = jnp.dot(dispatch, tokens[0], preferred_element_type=F32)
    slot_out[...] = own_slots.reshape(slot_out.shape).astype(BF16)

    pl.semaphore_wait(barrier, len(peers))

    def send_slots(landing, sem):
        for k in far_first:
            to = in_plane(k)
            remote(slot_out.at[to], landing, send_sem.at[0], sem, at_plane(to)).start()
        pltpu.make_async_copy(slot_out.at[plane], landing, sem).start()

    for number, (low, high) in enumerate(chunks):

        @pl.when(jnp.logical_and(plane >= low, plane < high))
        def _():
            send_slots(slots[number].at[place * (high - low) + plane - low], recv_sem.at[number])

    top = jnp.max(logits, axis=0, keepdims=True)
    weight = jnp.exp(logits - top)
    combine = (weight / jnp.sum(weight, axis=0, keepdims=True)).astype(BF16)
    is_first = plane < CUTS[1]

    @pl.when(is_first)
    def _():
        combine_ref[...] = (
            jnp.broadcast_to(combine[:, None, :], (planes, side, combine.shape[1]))
            .reshape(planes * side, combine.shape[1])
            .T
        )

    @pl.when(jnp.logical_not(is_first))
    def _():
        combine_ref[...] = jnp.concatenate(
            [combine, jnp.zeros((planes * (side - 1), combine.shape[1]), BF16)]
        ).T
        expert_ref[planes:] = jnp.zeros((planes * (side - 1), expert_ref.shape[1]), BF16)


    def spread(number):
        low, high = chunks[number]
        block = slots[number].at[pl.ds(place * (high - low), high - low)]
        wait_for(block, recv_sem.at[number])
        for k in range(1, side):
            remote(
                block, block, send_sem.at[1 + number], recv_sem.at[count + number], at_place(in_side(k))
            ).start()

    def send_direct():
        here, sem = direct.at[me], recv_sem.at[2 * count]
        for target in range(CUTS[1]):
            for k in range(1, side):
                to = in_side(k)
                own = partial[0].at[to * CUTS[1] + target]
                remote(own, here, send_sem.at[1 + count], sem, target * side + to).start()
            own = partial[0].at[place * CUTS[1] + target]

            @pl.when(plane == target)
            def _():
                pltpu.make_async_copy(own, here, sem).start()

            @pl.when(plane != target)
            def _():
                remote(own, here, send_sem.at[1 + count], sem, target * side + place).start()

    def experts(number):
        low, high = chunks[number]
        rows = high - low
        wait_for(slots[number].at[pl.ds(0, (side - 1) * rows)], recv_sem.at[count + number])
        hidden = jnp.dot(
            slots[number][...].reshape(side * rows, -1), w_in[...], preferred_element_type=F32
        )
        hidden = jax.nn.gelu(hidden).astype(BF16)
        out = jnp.dot(hidden, w_out[...], preferred_element_type=F32)
        partial[number][...] = out.reshape(partial[number].shape).astype(BF16)
        if number == 0:
            return send_direct()
        block = scattered[number].at[pl.ds(place * rows, rows)]
        sem = recv_sem.at[2 * count + number]
        for k in range(1, side):
            to = in_side(k)
            remote(
                partial[number].at[pl.ds(to * rows, rows)], block, send_sem.at[1 + count + number], sem, at_place(to)
            ).start()
        pltpu.make_async_copy(partial[number].at[pl.ds(place * rows, rows)], block, sem).start()

    def finish(number):
        low, high = chunks[number]
        rows = high - low
        wait_for(scattered[number], recv_sem.at[2 * count + number])
        total = jnp.zeros((rows * 2, scattered[number].shape[2]), F32)
        for k in range(side):
            part = scattered[number][k * rows : (k + 1) * rows]
            total = total + part.reshape(total.shape).astype(F32)
        expert_out[low:high] = total.astype(BF16).reshape(rows, 2, -1)
        for target in range(low, high):
            own = expert_out.at[target]

            @pl.when(plane == target)
            def _():
                pltpu.make_async_copy(own, expert_in.at[plane], recv_sem.at[3 * count]).start()

            @pl.when(plane != target)
            def _():
                remote(
                    own, expert_in.at[plane], send_sem.at[1 + 2 * count], recv_sem.at[3 * count], at_plane(target)
                ).start()

    spread(0)
    spread(1)
    spread(2)
    load_in.wait()
    load_out.wait()
    experts(0)
    experts(1)
    experts(2)
    finish(1)
    finish(2)

    @pl.when(is_first)
    def _():
        wait_for(direct, recv_sem.at[2 * count])
        expert_ref[...] = direct[...].reshape(expert_ref.shape)

    @pl.when(jnp.logical_not(is_first))
    def _():
        wait_for(expert_in, recv_sem.at[3 * count])
        expert_ref[:planes] = expert_in[...].reshape(planes, -1)

    wait_for(slot_out.at[pl.ds(0, planes - 1)], send_sem.at[0])
    for number, (low, high) in enumerate(chunks):
        others = pl.ds(0, (side - 1) * (high - low))
        wait_for(slots[number].at[others], send_sem.at[1 + number])
        if number > 0:
            wait_for(partial[number].at[others], send_sem.at[1 + count + number])

    @pl.when(is_first)
    def _():
        wait_for(partial[0].at[pl.ds(0, side * CUTS[1] - 1)], send_sem.at[1 + count])
        wait_for(expert_out.at[pl.ds(0, planes - CUTS[1])], send_sem.at[1 + 2 * count])

    @pl.when(jnp.logical_not(is_first))
    def _():
        wait_for(partial[0], send_sem.at[1 + count])
        wait_for(expert_out.at[pl.ds(0, planes - CUTS[1] - 1)], send_sem.at[1 + 2 * count])


def on_device(tokens, slot_weight, w_in, w_out, *, devices):
    images, patches, width = tokens.shape
    experts = slot_weight.shape[1]
    units = w_in.shape[1]
    planes = experts
    side = devices // planes
    dma = pltpu.SemaphoreType.DMA

    def rows(count):
        return pltpu.VMEM((count, 2, width // 2), BF16)

    vmem = pl.BlockSpec(memory_space=pltpu.VMEM)
    hbm = pl.BlockSpec(memory_space=pltpu.HBM)
    combine, expert_out = pl.pallas_call(
        functools.partial(kernel, planes, side),
        out_shape=[
            pltpu.VMEM((patches, devices), BF16),
            pltpu.VMEM((devices, width), BF16),
        ],
        in_specs=[hbm, hbm, hbm, hbm],
        out_specs=[vmem, vmem],
        scratch_shapes=[
            pltpu.VMEM((experts, width), BF16),
            pltpu.VMEM(tokens.shape, BF16),
            pltpu.VMEM((width, units), BF16),
            pltpu.VMEM((units, width), BF16),
            rows(planes),
            rows(devices),
            rows(devices),
            rows(devices),
            rows(devices),
            rows(planes),
            rows(planes),
            dma((4,)),
            dma((2 + 2 * len(CUTS),)),
            dma((1 + 3 * len(CUTS),)),
        ],
        compiler_params=pltpu.CompilerParams(
            collective_id=0, has_side_effects=True, vmem_limit_bytes=60 * 1024 * 1024
        ),
        cost_estimate=pl.CostEstimate(
            flops=2 * 2 * devices * width * units, bytes_accessed=4 * width * units, transcendentals=0
        ),
    )(tokens, slot_weight.T, w_in, w_out)
    mixed = jnp.dot(combine, expert_out, preferred_element_type=F32)
    return mixed.astype(BF16).reshape(tokens.shape)


def solution(mesh):
    in_specs = (
        P(("rep", "expert"), None, None),
        P("rep", None),
        P(None, "expert"),
        P("expert", None),
    )
    out_specs = P(("rep", "expert"), None, None)
    step = functools.partial(on_device, devices=mesh.shape["expert"])
    return jax.shard_map(step, mesh=mesh, in_specs=in_specs, out_specs=out_specs, check_vma=False)
```

```python
import functools

import jax
import jax.numpy as jnp
from jax import lax
from jax.experimental import pallas as pl
from jax.experimental.pallas import tpu as pltpu
from jax.sharding import PartitionSpec as P

BF16 = jnp.bfloat16
F32 = jnp.float32
CORES = 2
CUTS = (0, 2, 4)
PLACE_ORDER = (1, 0, 3, 2, 7, 6, 5, 4)
MIX_PARTS = 4
SIDE_ORDER = ((2, 0), (2, 1), (1, 0), (3, 0), (1, 1), (3, 1), (0, 1))


def remote(src, dst, send_sem, recv_sem, target):
    return pltpu.make_async_remote_copy(
        src_ref=src,
        dst_ref=dst,
        send_sem=send_sem,
        recv_sem=recv_sem,
        device_id={"expert": target},
        device_id_type=pl.DeviceIdType.MESH,
    )


def wait_for(rows, sem):
    pltpu.make_async_copy(rows, rows, sem).wait()


def kernel(
    planes,
    side,
    tokens_hbm,
    slot_hbm,
    w_in_hbm,
    w_out_hbm,
    combine_ref,
    expert_ref,
    slot_weight,
    tokens,
    w_in,
    w_out,
    slot_out,
    slots,
    partial,
    scattered,
    direct,
    expert_out,
    expert_in,
    load_sem,
    send_sem,
    recv_sem,
):
    chunks = list(zip(CUTS, CUTS[1:] + (planes,)))
    count = len(chunks)
    slots, partial, scattered = (
        [ref.at[pl.ds(side * low, side * (high - low))] for low, high in chunks]
        for ref in (slots, partial, scattered)
    )
    me = lax.axis_index("expert")
    place = lax.rem(me, side)
    plane = lax.div(me, side)

    def in_plane(step):
        return lax.rem(plane + step, planes)

    def at_plane(other):
        return other * side + place

    core = lax.rem(place, CORES)
    columns = side // CORES

    def in_side(step):
        column, other = SIDE_ORDER[step - 1]
        column = lax.rem(lax.div(place, CORES) + column, columns)
        return column * CORES + (1 - core if other else core)

    def at_place(other):
        return plane * side + other

    load_tokens = pltpu.make_async_copy(tokens_hbm, tokens, load_sem.at[0])
    load_slot = pltpu.make_async_copy(slot_hbm, slot_weight, load_sem.at[3])
    load_in = pltpu.make_async_copy(w_in_hbm, w_in, load_sem.at[1])
    load_out = pltpu.make_async_copy(w_out_hbm, w_out, load_sem.at[2])
    barrier = pltpu.get_barrier_semaphore()
    far_first = sorted(range(1, planes), key=lambda k: -min(k, planes - k))
    peers = [at_plane(in_plane(k)) for k in far_first]
    peers += [at_place(in_side(k)) for k in range(1, side)]
    for peer in peers:
        pl.semaphore_signal(
            barrier, inc=1, device_id={"expert": peer}, device_id_type=pl.DeviceIdType.MESH
        )
    load_slot.start()
    load_tokens.start()
    load_in.start()
    load_out.start()

    load_slot.wait()
    load_tokens.wait()
    logits = lax.dot_general(
        slot_weight[...], tokens[0], (((1,), (1,)), ((), ())), preferred_element_type=F32
    )
    top = jnp.max(logits, axis=1, keepdims=True)
    weight = jnp.exp(logits - top)
    dispatch = (weight / jnp.sum(weight, axis=1, keepdims=True)).astype(BF16)
    own_slots = jnp.dot(dispatch, tokens[0], preferred_element_type=F32)
    slot_out[...] = own_slots.reshape(slot_out.shape).astype(BF16)

    pl.semaphore_wait(barrier, len(peers))

    def send_slots(landing, sem):
        for k in far_first:
            to = in_plane(k)
            remote(slot_out.at[to], landing, send_sem.at[0], sem, at_plane(to)).start()
        pltpu.make_async_copy(slot_out.at[plane], landing, sem).start()

    for number, (low, high) in enumerate(chunks):

        @pl.when(jnp.logical_and(plane >= low, plane < high))
        def _():
            send_slots(slots[number].at[place * (high - low) + plane - low], recv_sem.at[number])

    top = jnp.max(logits, axis=0, keepdims=True)
    weight = jnp.exp(logits - top)
    combine = (weight / jnp.sum(weight, axis=0, keepdims=True)).astype(BF16)
    is_first = plane < CUTS[1]

    @pl.when(is_first)
    def _():
        combine_ref[...] = (
            jnp.broadcast_to(combine[:, None, :], (planes, side, combine.shape[1]))
            .reshape(planes * side, combine.shape[1])
            .T
        )

    @pl.when(jnp.logical_not(is_first))
    def _():
        combine_ref[...] = jnp.concatenate(
            [combine, jnp.zeros((planes * (side - 1), combine.shape[1]), BF16)]
        ).T
        expert_ref[planes:] = jnp.zeros((planes * (side - 1), expert_ref.shape[1]), BF16)


    def spread(number):
        low, high = chunks[number]
        block = slots[number].at[pl.ds(place * (high - low), high - low)]
        wait_for(block, recv_sem.at[number])
        for k in range(1, side):
            remote(
                block, block, send_sem.at[1 + number], recv_sem.at[count + number], at_place(in_side(k))
            ).start()

    def send_direct():
        here, sem = direct.at[me], recv_sem.at[2 * count]
        for target in range(CUTS[1]):
            for to in PLACE_ORDER:
                own = partial[0].at[to * CUTS[1] + target]
                is_own = me == target * side + to

                @pl.when(is_own)
                def _():
                    pltpu.make_async_copy(own, here, sem).start()

                @pl.when(jnp.logical_not(is_own))
                def _():
                    remote(own, here, send_sem.at[1 + count], sem, target * side + to).start()

    def experts(number):
        low, high = chunks[number]
        rows = high - low
        wait_for(slots[number].at[pl.ds(0, (side - 1) * rows)], recv_sem.at[count + number])
        hidden = jnp.dot(
            slots[number][...].reshape(side * rows, -1), w_in[...], preferred_element_type=F32
        )
        hidden = jax.nn.gelu(hidden).astype(BF16)
        out = jnp.dot(hidden, w_out[...], preferred_element_type=F32)
        partial[number][...] = out.reshape(partial[number].shape).astype(BF16)
        if number == 0:
            return send_direct()
        block = scattered[number].at[pl.ds(place * rows, rows)]
        sem = recv_sem.at[2 * count + number]
        for k in range(1, side):
            to = in_side(k)
            remote(
                partial[number].at[pl.ds(to * rows, rows)], block, send_sem.at[1 + count + number], sem, at_place(to)
            ).start()
        pltpu.make_async_copy(partial[number].at[pl.ds(place * rows, rows)], block, sem).start()

    def finish(number):
        low, high = chunks[number]
        rows = high - low
        wait_for(scattered[number], recv_sem.at[2 * count + number])
        total = jnp.zeros((rows * 2, scattered[number].shape[2]), F32)
        for k in range(side):
            part = scattered[number][k * rows : (k + 1) * rows]
            total = total + part.reshape(total.shape).astype(F32)
        expert_out[low:high] = total.astype(BF16).reshape(rows, 2, -1)
        for target in range(low, high):
            own = expert_out.at[target]

            @pl.when(plane == target)
            def _():
                pltpu.make_async_copy(own, expert_in.at[plane], recv_sem.at[3 * count]).start()

            @pl.when(plane != target)
            def _():
                remote(
                    own, expert_in.at[plane], send_sem.at[1 + 2 * count], recv_sem.at[3 * count], at_plane(target)
                ).start()

    spread(0)
    spread(1)
    spread(2)
    load_in.wait()
    load_out.wait()
    experts(0)
    experts(1)
    experts(2)
    finish(1)
    finish(2)

    @pl.when(is_first)
    def _():
        wait_for(direct, recv_sem.at[2 * count])
        expert_ref[...] = direct[...].reshape(expert_ref.shape)

    @pl.when(jnp.logical_not(is_first))
    def _():
        wait_for(expert_in, recv_sem.at[3 * count])
        expert_ref[:planes] = expert_in[...].reshape(planes, -1)

    wait_for(slot_out.at[pl.ds(0, planes - 1)], send_sem.at[0])
    for number, (low, high) in enumerate(chunks):
        others = pl.ds(0, (side - 1) * (high - low))
        wait_for(slots[number].at[others], send_sem.at[1 + number])
        if number > 0:
            wait_for(partial[number].at[others], send_sem.at[1 + count + number])

    @pl.when(is_first)
    def _():
        wait_for(partial[0].at[pl.ds(0, side * CUTS[1] - 1)], send_sem.at[1 + count])
        wait_for(expert_out.at[pl.ds(0, planes - CUTS[1])], send_sem.at[1 + 2 * count])

    @pl.when(jnp.logical_not(is_first))
    def _():
        wait_for(partial[0], send_sem.at[1 + count])
        wait_for(expert_out.at[pl.ds(0, planes - CUTS[1] - 1)], send_sem.at[1 + 2 * count])


def on_device(tokens, slot_weight, w_in, w_out, *, devices):
    images, patches, width = tokens.shape
    experts = slot_weight.shape[1]
    units = w_in.shape[1]
    planes = experts
    side = devices // planes
    dma = pltpu.SemaphoreType.DMA

    def rows(count):
        return pltpu.VMEM((count, 2, width // 2), BF16)

    vmem = pl.BlockSpec(memory_space=pltpu.VMEM)
    hbm = pl.BlockSpec(memory_space=pltpu.HBM)
    combine, expert_out = pl.pallas_call(
        functools.partial(kernel, planes, side),
        out_shape=[
            pltpu.VMEM((patches, devices), BF16),
            pltpu.VMEM((devices, width), BF16),
        ],
        in_specs=[hbm, hbm, hbm, hbm],
        out_specs=[vmem, vmem],
        scratch_shapes=[
            pltpu.VMEM((experts, width), BF16),
            pltpu.VMEM(tokens.shape, BF16),
            pltpu.VMEM((width, units), BF16),
            pltpu.VMEM((units, width), BF16),
            rows(planes),
            rows(devices),
            rows(devices),
            rows(devices),
            rows(devices),
            rows(planes),
            rows(planes),
            dma((4,)),
            dma((2 + 2 * len(CUTS),)),
            dma((1 + 3 * len(CUTS),)),
        ],
        compiler_params=pltpu.CompilerParams(
            collective_id=0, has_side_effects=True, vmem_limit_bytes=60 * 1024 * 1024
        ),
        cost_estimate=pl.CostEstimate(
            flops=2 * 2 * devices * width * units, bytes_accessed=4 * width * units, transcendentals=0
        ),
    )(tokens, slot_weight.T, w_in, w_out)
    part_rows = patches // MIX_PARTS

    def mix(combine_ref, expert_ref, out_hbm, out, sem):
        parts = [pl.ds(part * part_rows, part_rows) for part in range(MIX_PARTS)]
        copies = [
            pltpu.make_async_copy(out.at[part], out_hbm.at[0, part], sem.at[number])
            for number, part in enumerate(parts)
        ]
        for part, copy in zip(parts, copies):
            out[part] = jnp.dot(
                combine_ref[part], expert_ref[...], preferred_element_type=F32
            ).astype(BF16)
            copy.start()
        for copy in copies:
            copy.wait()

    return pl.pallas_call(
        mix,
        out_shape=jax.ShapeDtypeStruct(tokens.shape, BF16),
        in_specs=[vmem, vmem],
        out_specs=hbm,
        scratch_shapes=[pltpu.VMEM((patches, width), BF16), dma((MIX_PARTS,))],
        compiler_params=pltpu.CompilerParams(vmem_limit_bytes=8 * 1024 * 1024),
    )(combine, expert_out)


def solution(mesh):
    in_specs = (
        P(("rep", "expert"), None, None),
        P("rep", None),
        P(None, "expert"),
        P("expert", None),
    )
    out_specs = P(("rep", "expert"), None, None)
    step = functools.partial(on_device, devices=mesh.shape["expert"])
    return jax.shard_map(step, mesh=mesh, in_specs=in_specs, out_specs=out_specs, check_vma=False)
```

```python
import functools

import jax
import jax.numpy as jnp
from jax import lax
from jax.experimental import pallas as pl
from jax.experimental.pallas import tpu as pltpu
from jax.sharding import PartitionSpec as P

BF16 = jnp.bfloat16
F32 = jnp.float32
CORES = 2
LATE = (6, 12)
CUTS = (0, 2, 4)
PLACE_ORDER = (1, 0, 3, 2, 7, 6, 5, 4)
MIX_PARTS = 4
SIDE_ORDER = ((2, 0), (2, 1), (1, 0), (3, 0), (1, 1), (3, 1), (0, 1))


def remote(src, dst, send_sem, recv_sem, target):
    return pltpu.make_async_remote_copy(
        src_ref=src,
        dst_ref=dst,
        send_sem=send_sem,
        recv_sem=recv_sem,
        device_id={"expert": target},
        device_id_type=pl.DeviceIdType.MESH,
    )


def wait_for(rows, sem):
    pltpu.make_async_copy(rows, rows, sem).wait()


def kernel(
    planes,
    side,
    tokens_hbm,
    slot_hbm,
    w_in_hbm,
    w_out_hbm,
    combine_ref,
    expert_ref,
    slot_weight,
    tokens,
    w_in,
    w_out,
    slot_out,
    slots,
    partial,
    scattered,
    direct,
    expert_out,
    expert_in,
    load_sem,
    send_sem,
    recv_sem,
):
    chunks = list(zip(CUTS, CUTS[1:] + (planes,)))
    count = len(chunks)
    slots, partial, scattered = (
        [ref.at[pl.ds(side * low, side * (high - low))] for low, high in chunks]
        for ref in (slots, partial, scattered)
    )
    me = lax.axis_index("expert")
    place = lax.rem(me, side)
    plane = lax.div(me, side)

    def in_plane(step):
        return lax.rem(plane + step, planes)

    def at_plane(other):
        return other * side + place

    core = lax.rem(place, CORES)
    columns = side // CORES

    def in_side(step):
        column, other = SIDE_ORDER[step - 1]
        column = lax.rem(lax.div(place, CORES) + column, columns)
        return column * CORES + (1 - core if other else core)

    def at_place(other):
        return plane * side + other

    load_tokens = pltpu.make_async_copy(tokens_hbm, tokens, load_sem.at[0])
    load_slot = pltpu.make_async_copy(slot_hbm, slot_weight, load_sem.at[3])
    load_in = pltpu.make_async_copy(w_in_hbm, w_in, load_sem.at[1])
    load_out = pltpu.make_async_copy(w_out_hbm, w_out, load_sem.at[2])
    barrier = pltpu.get_barrier_semaphore()
    far_first = sorted(range(1, planes), key=lambda k: -min(k, planes - k))
    peers = [at_plane(in_plane(k)) for k in far_first]
    peers += [at_place(in_side(k)) for k in range(1, side)]
    for peer in peers:
        pl.semaphore_signal(
            barrier, inc=1, device_id={"expert": peer}, device_id_type=pl.DeviceIdType.MESH
        )
    load_slot.start()
    load_tokens.start()
    load_in.start()
    load_out.start()

    load_slot.wait()
    load_tokens.wait()
    logits = lax.dot_general(
        slot_weight[...], tokens[0], (((1,), (1,)), ((), ())), preferred_element_type=F32
    )
    top = jnp.max(logits, axis=1, keepdims=True)
    weight = jnp.exp(logits - top)
    dispatch = (weight / jnp.sum(weight, axis=1, keepdims=True)).astype(BF16)
    own_slots = jnp.dot(dispatch, tokens[0], preferred_element_type=F32)
    slot_out[...] = own_slots.reshape(slot_out.shape).astype(BF16)

    pl.semaphore_wait(barrier, len(peers))

    def send_slots(landing, sem):
        for k in far_first:
            to = in_plane(k)
            remote(slot_out.at[to], landing, send_sem.at[0], sem, at_plane(to)).start()
        pltpu.make_async_copy(slot_out.at[plane], landing, sem).start()

    for number, (low, high) in enumerate(chunks):

        @pl.when(jnp.logical_and(plane >= low, plane < high))
        def _():
            send_slots(slots[number].at[place * (high - low) + plane - low], recv_sem.at[number])

    top = jnp.max(logits, axis=0, keepdims=True)
    weight = jnp.exp(logits - top)
    combine = (weight / jnp.sum(weight, axis=0, keepdims=True)).astype(BF16)
    is_first = plane < CUTS[1]

    @pl.when(is_first)
    def _():
        combine_ref[...] = (
            jnp.broadcast_to(combine[:, None, :], (planes, side, combine.shape[1]))
            .reshape(planes * side, combine.shape[1])
            .T
        )

    @pl.when(jnp.logical_not(is_first))
    def _():
        combine_ref[...] = jnp.concatenate(
            [combine, jnp.zeros((planes * (side - 1), combine.shape[1]), BF16)]
        ).T
        expert_ref[planes:] = jnp.zeros((planes * (side - 1), expert_ref.shape[1]), BF16)


    def spread(number):
        low, high = chunks[number]
        block = slots[number].at[pl.ds(place * (high - low), high - low)]
        wait_for(block, recv_sem.at[number])
        for k in range(1, side):
            remote(
                block, block, send_sem.at[1 + number], recv_sem.at[count + number], at_place(in_side(k))
            ).start()

    def send_direct():
        is_late = jnp.logical_and(plane >= LATE[0], plane < LATE[1])
        here, sem = direct.at[me], recv_sem.at[jnp.where(is_late, 2 * count, 3 * count + 1)]
        for target in range(CUTS[1]):
            for to in PLACE_ORDER:
                own = partial[0].at[to * CUTS[1] + target]
                is_own = me == target * side + to

                @pl.when(is_own)
                def _():
                    pltpu.make_async_copy(own, here, sem).start()

                @pl.when(jnp.logical_not(is_own))
                def _():
                    remote(own, here, send_sem.at[1 + count], sem, target * side + to).start()

    def experts(number):
        low, high = chunks[number]
        rows = high - low
        wait_for(slots[number].at[pl.ds(0, (side - 1) * rows)], recv_sem.at[count + number])
        hidden = jnp.dot(
            slots[number][...].reshape(side * rows, -1), w_in[...], preferred_element_type=F32
        )
        hidden = jax.nn.gelu(hidden).astype(BF16)
        out = jnp.dot(hidden, w_out[...], preferred_element_type=F32)
        partial[number][...] = out.reshape(partial[number].shape).astype(BF16)
        if number == 0:
            return send_direct()
        block = scattered[number].at[pl.ds(place * rows, rows)]
        sem = recv_sem.at[2 * count + number]
        for k in range(1, side):
            to = in_side(k)
            remote(
                partial[number].at[pl.ds(to * rows, rows)], block, send_sem.at[1 + count + number], sem, at_place(to)
            ).start()
        pltpu.make_async_copy(partial[number].at[pl.ds(place * rows, rows)], block, sem).start()

    def finish(number):
        low, high = chunks[number]
        rows = high - low
        wait_for(scattered[number], recv_sem.at[2 * count + number])
        total = jnp.zeros((rows * 2, scattered[number].shape[2]), F32)
        for k in range(side):
            part = scattered[number][k * rows : (k + 1) * rows]
            total = total + part.reshape(total.shape).astype(F32)
        expert_out[low:high] = total.astype(BF16).reshape(rows, 2, -1)
        for target in range(low, high):
            own = expert_out.at[target]

            @pl.when(plane == target)
            def _():
                pltpu.make_async_copy(own, expert_in.at[plane], recv_sem.at[3 * count]).start()

            @pl.when(plane != target)
            def _():
                remote(
                    own, expert_in.at[plane], send_sem.at[1 + 2 * count], recv_sem.at[3 * count], at_plane(target)
                ).start()

    spread(0)
    spread(1)
    spread(2)
    load_in.wait()
    load_out.wait()
    experts(0)
    experts(1)
    experts(2)
    finish(1)
    finish(2)

    wait_for(slot_out.at[pl.ds(0, planes - 1)], send_sem.at[0])
    for number, (low, high) in enumerate(chunks):
        others = pl.ds(0, (side - 1) * (high - low))
        wait_for(slots[number].at[others], send_sem.at[1 + number])
        if number > 0:
            wait_for(partial[number].at[others], send_sem.at[1 + count + number])

    @pl.when(is_first)
    def _():
        wait_for(partial[0].at[pl.ds(0, side * CUTS[1] - 1)], send_sem.at[1 + count])
        wait_for(expert_out.at[pl.ds(0, planes - CUTS[1])], send_sem.at[1 + 2 * count])

    @pl.when(jnp.logical_not(is_first))
    def _():
        wait_for(partial[0], send_sem.at[1 + count])
        wait_for(expert_out.at[pl.ds(0, planes - CUTS[1] - 1)], send_sem.at[1 + 2 * count])

    @pl.when(is_first)
    def _():
        soon = planes - LATE[1] + LATE[0]
        wait_for(direct.at[pl.ds(0, soon * side)], recv_sem.at[3 * count + 1])
        for low, high in ((0, LATE[0]), (LATE[1], planes)):
            part = slice(low * side, high * side)
            expert_ref[part] = direct[part].reshape((high - low) * side, -1)
        part = slice(LATE[0] * side, LATE[1] * side)
        wait_for(direct.at[pl.ds(part.start, part.stop - part.start)], recv_sem.at[2 * count])
        expert_ref[part] = direct[part].reshape(part.stop - part.start, -1)

    @pl.when(jnp.logical_not(is_first))
    def _():
        wait_for(expert_in, recv_sem.at[3 * count])
        expert_ref[:planes] = expert_in[...].reshape(planes, -1)


def on_device(tokens, slot_weight, w_in, w_out, *, devices):
    images, patches, width = tokens.shape
    experts = slot_weight.shape[1]
    units = w_in.shape[1]
    planes = experts
    side = devices // planes
    dma = pltpu.SemaphoreType.DMA

    def rows(count):
        return pltpu.VMEM((count, 2, width // 2), BF16)

    vmem = pl.BlockSpec(memory_space=pltpu.VMEM)
    hbm = pl.BlockSpec(memory_space=pltpu.HBM)
    combine, expert_out = pl.pallas_call(
        functools.partial(kernel, planes, side),
        out_shape=[
            pltpu.VMEM((patches, devices), BF16),
            pltpu.VMEM((devices, width), BF16),
        ],
        in_specs=[hbm, hbm, hbm, hbm],
        out_specs=[vmem, vmem],
        scratch_shapes=[
            pltpu.VMEM((experts, width), BF16),
            pltpu.VMEM(tokens.shape, BF16),
            pltpu.VMEM((width, units), BF16),
            pltpu.VMEM((units, width), BF16),
            rows(planes),
            rows(devices),
            rows(devices),
            rows(devices),
            rows(devices),
            rows(planes),
            rows(planes),
            dma((4,)),
            dma((2 + 2 * len(CUTS),)),
            dma((2 + 3 * len(CUTS),)),
        ],
        compiler_params=pltpu.CompilerParams(
            collective_id=0, has_side_effects=True, vmem_limit_bytes=60 * 1024 * 1024
        ),
        cost_estimate=pl.CostEstimate(
            flops=2 * 2 * devices * width * units, bytes_accessed=4 * width * units, transcendentals=0
        ),
    )(tokens, slot_weight.T, w_in, w_out)
    part_rows = patches // MIX_PARTS

    def mix(combine_ref, expert_ref, out_hbm, out, sem):
        parts = [pl.ds(part * part_rows, part_rows) for part in range(MIX_PARTS)]
        copies = [
            pltpu.make_async_copy(out.at[part], out_hbm.at[0, part], sem.at[number])
            for number, part in enumerate(parts)
        ]
        for part, copy in zip(parts, copies):
            out[part] = jnp.dot(
                combine_ref[part], expert_ref[...], preferred_element_type=F32
            ).astype(BF16)
            copy.start()
        for copy in copies:
            copy.wait()

    return pl.pallas_call(
        mix,
        out_shape=jax.ShapeDtypeStruct(tokens.shape, BF16),
        in_specs=[vmem, vmem],
        out_specs=hbm,
        scratch_shapes=[pltpu.VMEM((patches, width), BF16), dma((MIX_PARTS,))],
        compiler_params=pltpu.CompilerParams(vmem_limit_bytes=8 * 1024 * 1024),
    )(combine, expert_out)


def solution(mesh):
    in_specs = (
        P(("rep", "expert"), None, None),
        P("rep", None),
        P(None, "expert"),
        P("expert", None),
    )
    out_specs = P(("rep", "expert"), None, None)
    step = functools.partial(on_device, devices=mesh.shape["expert"])
    return jax.shard_map(step, mesh=mesh, in_specs=in_specs, out_specs=out_specs, check_vma=False)
```

```python
import functools

import jax
import jax.numpy as jnp
from jax import lax
from jax.experimental import pallas as pl
from jax.experimental.pallas import tpu as pltpu
from jax.sharding import PartitionSpec as P

BF16 = jnp.bfloat16
F32 = jnp.float32
CORES = 2
CUTS = (0, 2, 4)
PLACE_ORDER = (1, 0, 3, 2, 7, 6, 5, 4)
MIX_PARTS = 4
SIDE_ORDER = ((2, 0), (2, 1), (3, 0), (1, 0), (3, 1), (1, 1), (0, 1))


def remote(src, dst, send_sem, recv_sem, target):
    return pltpu.make_async_remote_copy(
        src_ref=src,
        dst_ref=dst,
        send_sem=send_sem,
        recv_sem=recv_sem,
        device_id={"expert": target},
        device_id_type=pl.DeviceIdType.MESH,
    )


def wait_for(rows, sem):
    pltpu.make_async_copy(rows, rows, sem).wait()


def kernel(
    planes,
    side,
    tokens_hbm,
    slot_hbm,
    w_in_hbm,
    w_out_hbm,
    combine_ref,
    expert_ref,
    slot_weight,
    tokens,
    w_in,
    w_out,
    slot_out,
    slots,
    partial,
    scattered,
    direct,
    expert_out,
    expert_in,
    load_sem,
    send_sem,
    recv_sem,
):
    chunks = list(zip(CUTS, CUTS[1:] + (planes,)))
    count = len(chunks)
    slots, partial, scattered = (
        [ref.at[pl.ds(side * low, side * (high - low))] for low, high in chunks]
        for ref in (slots, partial, scattered)
    )
    me = lax.axis_index("expert")
    place = lax.rem(me, side)
    plane = lax.div(me, side)

    def in_plane(step):
        return lax.rem(plane + step, planes)

    def at_plane(other):
        return other * side + place

    core = lax.rem(place, CORES)
    columns = side // CORES

    def in_side(step):
        column, other = SIDE_ORDER[step - 1]
        column = lax.rem(lax.div(place, CORES) + column, columns)
        return column * CORES + (1 - core if other else core)

    def at_place(other):
        return plane * side + other

    load_tokens = pltpu.make_async_copy(tokens_hbm, tokens, load_sem.at[0])
    load_slot = pltpu.make_async_copy(slot_hbm, slot_weight, load_sem.at[3])
    load_in = pltpu.make_async_copy(w_in_hbm, w_in, load_sem.at[1])
    load_out = pltpu.make_async_copy(w_out_hbm, w_out, load_sem.at[2])
    barrier = pltpu.get_barrier_semaphore()
    far_first = sorted(range(1, planes), key=lambda k: -min(k, planes - k))
    peers = [at_plane(in_plane(k)) for k in far_first]
    peers += [at_place(in_side(k)) for k in range(1, side)]
    for peer in peers:
        pl.semaphore_signal(
            barrier, inc=1, device_id={"expert": peer}, device_id_type=pl.DeviceIdType.MESH
        )
    load_slot.start()
    load_tokens.start()
    load_in.start()
    load_out.start()

    load_slot.wait()
    load_tokens.wait()
    logits = lax.dot_general(
        slot_weight[...], tokens[0], (((1,), (1,)), ((), ())), preferred_element_type=F32
    )
    top = jnp.max(logits, axis=1, keepdims=True)
    weight = jnp.exp(logits - top)
    dispatch = (weight / jnp.sum(weight, axis=1, keepdims=True)).astype(BF16)
    own_slots = jnp.dot(dispatch, tokens[0], preferred_element_type=F32)
    slot_out[...] = own_slots.reshape(slot_out.shape).astype(BF16)

    pl.semaphore_wait(barrier, len(peers))

    def send_slots(landing, sem):
        for k in far_first:
            to = in_plane(k)
            remote(slot_out.at[to], landing, send_sem.at[0], sem, at_plane(to)).start()
        pltpu.make_async_copy(slot_out.at[plane], landing, sem).start()

    for number, (low, high) in enumerate(chunks):

        @pl.when(jnp.logical_and(plane >= low, plane < high))
        def _():
            send_slots(slots[number].at[place * (high - low) + plane - low], recv_sem.at[number])

    top = jnp.max(logits, axis=0, keepdims=True)
    weight = jnp.exp(logits - top)
    combine = (weight / jnp.sum(weight, axis=0, keepdims=True)).astype(BF16)
    is_first = plane < CUTS[1]

    @pl.when(is_first)
    def _():
        combine_ref[...] = (
            jnp.broadcast_to(combine[:, None, :], (planes, side, combine.shape[1]))
            .reshape(planes * side, combine.shape[1])
            .T
        )

    @pl.when(jnp.logical_not(is_first))
    def _():
        combine_ref[...] = jnp.concatenate(
            [combine, jnp.zeros((planes * (side - 1), combine.shape[1]), BF16)]
        ).T
        expert_ref[planes:] = jnp.zeros((planes * (side - 1), expert_ref.shape[1]), BF16)


    def spread(number):
        low, high = chunks[number]
        block = slots[number].at[pl.ds(place * (high - low), high - low)]
        wait_for(block, recv_sem.at[number])
        for k in range(1, side):
            remote(
                block, block, send_sem.at[1 + number], recv_sem.at[count + number], at_place(in_side(k))
            ).start()

    def send_direct():
        here, sem = direct.at[me], recv_sem.at[2 * count]
        for target in range(CUTS[1]):
            for to in PLACE_ORDER:
                own = partial[0].at[to * CUTS[1] + target]
                is_own = me == target * side + to

                @pl.when(is_own)
                def _():
                    pltpu.make_async_copy(own, here, sem).start()

                @pl.when(jnp.logical_not(is_own))
                def _():
                    remote(own, here, send_sem.at[1 + count], sem, target * side + to).start()

    def experts(number):
        low, high = chunks[number]
        rows = high - low
        wait_for(slots[number].at[pl.ds(0, (side - 1) * rows)], recv_sem.at[count + number])
        hidden = jnp.dot(
            slots[number][...].reshape(side * rows, -1), w_in[...], preferred_element_type=F32
        )
        hidden = jax.nn.gelu(hidden).astype(BF16)
        out = jnp.dot(hidden, w_out[...], preferred_element_type=F32)
        partial[number][...] = out.reshape(partial[number].shape).astype(BF16)
        if number == 0:
            return send_direct()
        block = scattered[number].at[pl.ds(place * rows, rows)]
        sem = recv_sem.at[2 * count + number]
        for k in range(1, side):
            to = in_side(k)
            remote(
                partial[number].at[pl.ds(to * rows, rows)], block, send_sem.at[1 + count + number], sem, at_place(to)
            ).start()
        pltpu.make_async_copy(partial[number].at[pl.ds(place * rows, rows)], block, sem).start()

    def finish(number):
        low, high = chunks[number]
        rows = high - low
        wait_for(scattered[number], recv_sem.at[2 * count + number])
        total = jnp.zeros((rows * 2, scattered[number].shape[2]), F32)
        for k in range(side):
            part = scattered[number][k * rows : (k + 1) * rows]
            total = total + part.reshape(total.shape).astype(F32)
        expert_out[low:high] = total.astype(BF16).reshape(rows, 2, -1)
        for target in range(low, high):
            own = expert_out.at[target]

            @pl.when(plane == target)
            def _():
                pltpu.make_async_copy(own, expert_in.at[plane], recv_sem.at[3 * count]).start()

            @pl.when(plane != target)
            def _():
                remote(
                    own, expert_in.at[plane], send_sem.at[1 + 2 * count], recv_sem.at[3 * count], at_plane(target)
                ).start()

    spread(0)
    spread(1)
    spread(2)
    load_in.wait()
    load_out.wait()
    experts(0)
    experts(1)
    experts(2)
    finish(1)
    finish(2)

    @pl.when(is_first)
    def _():
        wait_for(direct, recv_sem.at[2 * count])
        expert_ref[...] = direct[...].reshape(expert_ref.shape)

    @pl.when(jnp.logical_not(is_first))
    def _():
        wait_for(expert_in, recv_sem.at[3 * count])
        expert_ref[:planes] = expert_in[...].reshape(planes, -1)

    wait_for(slot_out.at[pl.ds(0, planes - 1)], send_sem.at[0])
    for number, (low, high) in enumerate(chunks):
        others = pl.ds(0, (side - 1) * (high - low))
        wait_for(slots[number].at[others], send_sem.at[1 + number])
        if number > 0:
            wait_for(partial[number].at[others], send_sem.at[1 + count + number])

    @pl.when(is_first)
    def _():
        wait_for(partial[0].at[pl.ds(0, side * CUTS[1] - 1)], send_sem.at[1 + count])
        wait_for(expert_out.at[pl.ds(0, planes - CUTS[1])], send_sem.at[1 + 2 * count])

    @pl.when(jnp.logical_not(is_first))
    def _():
        wait_for(partial[0], send_sem.at[1 + count])
        wait_for(expert_out.at[pl.ds(0, planes - CUTS[1] - 1)], send_sem.at[1 + 2 * count])


def on_device(tokens, slot_weight, w_in, w_out, *, devices):
    images, patches, width = tokens.shape
    experts = slot_weight.shape[1]
    units = w_in.shape[1]
    planes = experts
    side = devices // planes
    dma = pltpu.SemaphoreType.DMA

    def rows(count):
        return pltpu.VMEM((count, 2, width // 2), BF16)

    vmem = pl.BlockSpec(memory_space=pltpu.VMEM)
    hbm = pl.BlockSpec(memory_space=pltpu.HBM)
    combine, expert_out = pl.pallas_call(
        functools.partial(kernel, planes, side),
        out_shape=[
            pltpu.VMEM((patches, devices), BF16),
            pltpu.VMEM((devices, width), BF16),
        ],
        in_specs=[hbm, hbm, hbm, hbm],
        out_specs=[vmem, vmem],
        scratch_shapes=[
            pltpu.VMEM((experts, width), BF16),
            pltpu.VMEM(tokens.shape, BF16),
            pltpu.VMEM((width, units), BF16),
            pltpu.VMEM((units, width), BF16),
            rows(planes),
            rows(devices),
            rows(devices),
            rows(devices),
            rows(devices),
            rows(planes),
            rows(planes),
            dma((4,)),
            dma((2 + 2 * len(CUTS),)),
            dma((1 + 3 * len(CUTS),)),
        ],
        compiler_params=pltpu.CompilerParams(
            collective_id=0, has_side_effects=True, vmem_limit_bytes=60 * 1024 * 1024
        ),
        cost_estimate=pl.CostEstimate(
            flops=2 * 2 * devices * width * units, bytes_accessed=4 * width * units, transcendentals=0
        ),
    )(tokens, slot_weight.T, w_in, w_out)
    part_rows = patches // MIX_PARTS

    def mix(combine_ref, expert_ref, out_hbm, out, sem):
        parts = [pl.ds(part * part_rows, part_rows) for part in range(MIX_PARTS)]
        copies = [
            pltpu.make_async_copy(out.at[part], out_hbm.at[0, part], sem.at[number])
            for number, part in enumerate(parts)
        ]
        for part, copy in zip(parts, copies):
            out[part] = jnp.dot(
                combine_ref[part], expert_ref[...], preferred_element_type=F32
            ).astype(BF16)
            copy.start()
        for copy in copies:
            copy.wait()

    return pl.pallas_call(
        mix,
        out_shape=jax.ShapeDtypeStruct(tokens.shape, BF16),
        in_specs=[vmem, vmem],
        out_specs=hbm,
        scratch_shapes=[pltpu.VMEM((patches, width), BF16), dma((MIX_PARTS,))],
        compiler_params=pltpu.CompilerParams(vmem_limit_bytes=8 * 1024 * 1024),
    )(combine, expert_out)


def solution(mesh):
    in_specs = (
        P(("rep", "expert"), None, None),
        P("rep", None),
        P(None, "expert"),
        P("expert", None),
    )
    out_specs = P(("rep", "expert"), None, None)
    step = functools.partial(on_device, devices=mesh.shape["expert"])
    return jax.shard_map(step, mesh=mesh, in_specs=in_specs, out_specs=out_specs, check_vma=False)
```
